512 devices in a mesh: grp: 32 (over z_lo, y), sp: 16 (over z_hi, x, core).
Axes of the slice: x: 4, y: 4, z: 16 (z_hi: 2, z_lo: 8; z = z_hi * 8 + z_lo), core: 2. Of those that a mesh axis runs over, the one named last changes fastest.
Arguments:
- active_qkv: bfloat16 [3, 3072, 6144], P(None, ('grp', 'sp')), may hold values from -8 to 8
- window_kv: bfloat16 [2, 24576, 6144], P(None, 'grp', 'sp'), may hold values from -8 to 8
- slot_owner: int32 [32], replicated, may hold values from 0 to 7, as said below
- oldest_slot: int32 [1], replicated, may hold values from 0 to 7
- timestep: int32 [1], replicated, may hold values from 0 to 49
- time_slopes: float32 [48], replicated, may hold values from 0.02 to 1
- gate_table: float32 [50, 6144], replicated, may hold values from 0.25 to 2
Outputs:
- attended: bfloat16 [3072, 6144], P(('grp', 'sp'))
- new_window: bfloat16 [2, 24576, 6144], P(None, 'grp', 'sp')
The draws below stay inside these ranges and needn't reach their ends.
Inputs may be any that keep to these rules, and one draw needn't show every extreme that they name: `slot_owner`: each of the 8 slots is held by exactly 4 groups, all in the same half of the groups; a group's slot depends only on its index mod 4 and on its half.
All inputs are finite; a program needn't handle non-finite values.
Results may differ from the reference program's by a relative error of at most 0.018.
Values may be sent and summed in bfloat16 or wider, within the bound.
A program may use at most 64 MiB of HBM per device.

```python
import math
import jax
import jax.numpy as jnp
from jax import lax

H = 48
HD = 128
D = 6144
WIN = 8
STEPS = 50
TOKG = 96
SPAN = 3072
CTOK = 768
N_GRP = 32


def draw_active_qkv(key, part):
    key = jax.random.fold_in(key, 1)
    scales = jnp.array([1.0, 1.0, 1.0 / 1.7], jnp.float32)[:, None, None]
    base = 1.7 * jax.random.truncated_normal(key, -8.0 / 1.7, 8.0 / 1.7, (3, SPAN, D), jnp.float32) * scales
    return base.astype(jnp.bfloat16)


def draw_window_kv(key, part):
    key = jax.random.fold_in(key, 2)
    scales = jnp.array([1.0, 1.0 / 1.7], jnp.float32)[:, None, None]
    total_rows = N_GRP * CTOK
    base = 1.7 * jax.random.truncated_normal(key, -8.0 / 1.7, 8.0 / 1.7, (2, total_rows, D), jnp.float32) * scales
    return base.astype(jnp.bfloat16)


def draw_slot_owner(key, part):
    key = jax.random.fold_in(key, 3)
    order = jax.random.permutation(key, WIN).astype(jnp.int32)
    group_ids = jnp.arange(N_GRP, dtype=jnp.int32)
    upper_half = (group_ids >= N_GRP // 2).astype(jnp.int32)
    position = upper_half * (WIN // 2) + jnp.mod(group_ids, WIN // 2)
    return order[position].astype(jnp.int32)


def setup_inputs(seed: int = 0) -> dict:
    arg_keys = jax.random.split(jax.random.key(seed), 8)
    return {
        "active_qkv": draw_active_qkv(jax.random.fold_in(arg_keys[7], 71), 0),
        "window_kv": draw_window_kv(jax.random.fold_in(arg_keys[7], 71), 0),
        "slot_owner": draw_slot_owner(jax.random.fold_in(arg_keys[7], 71), 0),
        "oldest_slot": jax.random.randint(arg_keys[3], (1,), 0, WIN).astype(jnp.int32),
        "timestep": jax.random.randint(arg_keys[4], (1,), 0, STEPS).astype(jnp.int32),
        "time_slopes": jnp.clip(jnp.exp(jax.random.uniform(arg_keys[5], (H,), jnp.float32, math.log(0.02), math.log(1.0))), 0.02, 1.0),
        "gate_table": jnp.clip(jax.random.uniform(arg_keys[6], (STEPS, D), jnp.float32, 0.25, 2.0), 0.25, 2.0),
    }


def reference(active_qkv, window_kv, slot_owner, oldest_slot, timestep, time_slopes, gate_table):
    scale = 1.0 / math.sqrt(HD)
    oldest = oldest_slot[0]
    ages = (WIN - jnp.mod(slot_owner - oldest, WIN)).astype(jnp.int32)
    queries = jnp.transpose(active_qkv[0].reshape(SPAN, H, HD), (1, 0, 2))
    count = CTOK + TOKG

    def group_keys(group):
        cached = lax.dynamic_slice_in_dim(window_kv, (group * CTOK).astype(jnp.int32), CTOK, 1)
        fresh = lax.dynamic_slice_in_dim(active_qkv[1:], (group * TOKG).astype(jnp.int32), TOKG, 1)
        keyset = jnp.concatenate([cached, fresh], axis=1)
        heads_kv = jnp.transpose(keyset.reshape(2, count, H, HD), (2, 0, 1, 3))
        age_row = jnp.concatenate([jnp.full((CTOK,), 1.0, jnp.float32) * ages[group].astype(jnp.float32), jnp.zeros((TOKG,), jnp.float32)])
        return (heads_kv, age_row)

    def lse_pass(group):
        heads_kv, age_row = group_keys(group)

        def per_head(items):
            query, pair, slope = items
            score = jnp.dot(query, pair[0].T, preferred_element_type=jnp.float32) * scale - slope * age_row[None, :]
            top = lax.optimization_barrier(jnp.max(score, axis=1))
            total = lax.optimization_barrier(jnp.sum(jnp.exp(score - top[:, None]), axis=1))
            return top + jnp.log(total)
        return lax.map(per_head, (queries, heads_kv, time_slopes))
    lses = lax.map(lse_pass, jnp.arange(N_GRP, dtype=jnp.int32))
    best = lax.optimization_barrier(jnp.max(lses, axis=0))

    def group_step(carry, group):
        numer, denom = carry
        heads_kv, age_row = group_keys(group)

        def per_head(items):
            query, pair, slope = items
            score = jnp.dot(query, pair[0].T, preferred_element_type=jnp.float32) * scale - slope * age_row[None, :]
            top = lax.optimization_barrier(jnp.max(score, axis=1))
            weight = jnp.exp(score - top[:, None])
            total = lax.optimization_barrier(jnp.sum(weight, axis=1))
            return (jnp.dot(weight.astype(jnp.bfloat16), pair[1], preferred_element_type=jnp.float32) / total[:, None]).astype(jnp.bfloat16)
        partial_value = lax.map(per_head, (queries, heads_kv, time_slopes))
        factor = jnp.exp(lses[group] - best)
        term = (factor[..., None] * partial_value.astype(jnp.float32)).astype(jnp.bfloat16)
        term = lax.optimization_barrier(term)
        return ((numer + term.astype(jnp.float32), denom + factor), None)
    start = (jnp.zeros((H, SPAN, HD), jnp.float32), jnp.zeros((H, SPAN), jnp.float32))
    (numer, denom), _ = lax.scan(group_step, start, jnp.arange(N_GRP, dtype=jnp.int32))
    combined = jnp.transpose(numer / denom[..., None], (1, 0, 2)).reshape(SPAN, D).astype(jnp.bfloat16)
    gate = gate_table[timestep[0]]
    attended = (gate[None, :] * combined.astype(jnp.float32)).astype(jnp.bfloat16)
    is_old = (slot_owner == oldest).astype(jnp.int32)
    before = (jnp.cumsum(is_old) - is_old).astype(jnp.int32)
    fresh_kv = active_qkv[1:]

    def rebuild(group):
        cached = lax.dynamic_slice_in_dim(window_kv, (group * CTOK).astype(jnp.int32), CTOK, 1)
        moved = lax.dynamic_slice_in_dim(fresh_kv, (before[group] * CTOK).astype(jnp.int32), CTOK, 1)
        return jnp.where(is_old[group] == 1, moved, cached)
    blocks = lax.map(rebuild, jnp.arange(N_GRP, dtype=jnp.int32))
    new_window = jnp.transpose(blocks, (1, 0, 2, 3)).reshape(2, N_GRP * CTOK, D)
    return (attended, new_window)
```

```python
import functools
import math

import jax
import jax.numpy as jnp
from jax import lax
from jax.experimental import pallas as pl
from jax.experimental.pallas import tpu as pltpu
from jax.sharding import PartitionSpec as P

HD = 128
WIN = 8
HEADS = 3
SHARE = HEADS * HD
ROWS = 96
CACHE = 768
NZ = 8
NY = 4
PACK = 4 * ROWS
LOG2E = math.log2(math.e)
COEF = LOG2E / math.sqrt(HD)
NONE = -1e30
MESH = pl.DeviceIdType.MESH
BF = jnp.bfloat16
F32 = jnp.float32


def lse2(*parts):
    top = functools.reduce(jnp.maximum, parts)
    return top + jnp.log2(sum(jnp.exp2(p - top) for p in parts))


def kernel(
    local_ref, win_ref, bias_ref, out_ref, moved_ref,
    qbuf, vt, va, opart, lpart, lrecv, wrelay, wfinal, zl_own,
    r1, r2, r3, relayed, zo_own, zo_recv, zo_out, zl_recv, zl_out, wz,
    zsend, zrecv, ysend, yrecv, y2send, y2recv,
    ls_sem, lr_sem, r1s, r1r, r2s, r2r, r3s, r3r,
    zos, zor, zls, zlr, ezs, ezr, eys, eyr, e2s, e2r, cp_sem,
):
    me = lax.axis_index("grp")
    z = me // NY
    y = me % NY
    yp = (y + 1) % NY
    ym = (y + 3) % NY
    y2 = (y + 2) % NY
    near = z // 4
    far = 1 - near

    def at(zz, yy):
        return {"grp": zz * NY + yy}

    def copy(src, dst, send, recv, dev):
        return pltpu.make_async_remote_copy(
            src_ref=src, dst_ref=dst, send_sem=send, recv_sem=recv,
            device_id=dev, device_id_type=MESH,
        )

    barrier = pltpu.get_barrier_semaphore()
    for step in range(1, NZ):
        pl.semaphore_signal(barrier, inc=1, device_id=at((z + step) % NZ, y), device_id_type=MESH)
    for step in range(1, NY):
        pl.semaphore_signal(barrier, inc=1, device_id=at(z, (y + step) % NY), device_id_type=MESH)
    pl.semaphore_wait(barrier, NZ - 1 + NY - 1)

    def z_copy(block, side):
        return copy(
            qbuf.at[y, block], qbuf.at[y, block], zsend.at[side, block], zrecv.at[block],
            at(z + 1 - 2 * side, y),
        )

    def y_copy(block, side):
        return copy(
            qbuf.at[y, block], qbuf.at[y, block], ysend.at[side, block], yrecv.at[side, block],
            at(z, ym if side else yp),
        )

    def y2_copy(block, odd):
        column = ym + odd * (yp - ym)
        return copy(
            qbuf.at[column, block], qbuf.at[column, block], y2send.at[block], y2recv.at[block],
            at(z, yp + odd * (ym - yp)),
        )

    def y_wait(block, side):
        column = yp if side else ym
        copy(
            qbuf.at[column, block], qbuf.at[column, block], ysend.at[side, block],
            yrecv.at[side, block], at(z, column),
        ).wait_recv()

    def y2_wait(block):
        copy(
            qbuf.at[y2, block], qbuf.at[y2, block], y2send.at[block], y2recv.at[block], at(z, yp)
        ).wait_recv()

    def z_wait(block):
        copy(
            qbuf.at[y, block], qbuf.at[y, block], zsend.at[0, block], zrecv.at[block], at(z, yp)
        ).wait_recv()

    def spread(block):
        y_copy(block, 0).start()
        y_copy(block, 1).start()

    def evict_z(half):
        rows = pl.ds(((z % 2) * NY + y) * ROWS, ROWS)
        return copy(
            local_ref.at[pl.ds(1, 2)], moved_ref.at[:, rows, :], ezs.at[half], ezr.at[z % 2],
            at(z // 2 + 4 * half, y),
        )

    def evict_own():
        rows = pl.ds(((z % 2) * NY + y) * ROWS, ROWS)
        return pltpu.make_async_copy(
            local_ref.at[pl.ds(1, 2)], moved_ref.at[:, rows, :], cp_sem
        )

    def evict_rows(which, column):
        return moved_ref.at[:, pl.ds((which * NY + column) * ROWS, ROWS), :]

    def evict_y(which, side):
        rows = evict_rows(which, y)
        return copy(
            rows, rows, eys.at[side, which], eyr.at[side, which], at(z, ym if side else yp)
        )

    def evict_y_wait(which, side):
        rows = evict_rows(which, yp if side else ym)
        copy(rows, rows, eys.at[side, which], eyr.at[side, which], at(z, yp)).wait_recv()

    def evict_y2(which):
        rows = evict_rows(which, yp if which else ym)
        return copy(rows, rows, e2s.at[which], e2r.at[which], at(z, ym if which else yp))

    def evict_y2_wait(which):
        rows = evict_rows(which, y2)
        copy(rows, rows, e2s.at[which], e2r.at[which], at(z, yp)).wait_recv()

    qbuf[y, z] = local_ref[0]

    @pl.when(z < NZ - 1)
    def _():
        z_copy(z, 0).start()

    @pl.when(z > 0)
    def _():
        z_copy(z, 1).start()

    spread(z)

    for h in range(HEADS):
        cols = slice(h * HD, (h + 1) * HD)
        vt[h, 0:HD, :] = win_ref[1, :, cols].astype(F32).T.astype(BF)
        vt[h, HD : HD + 16, :] = jnp.ones((16, CACHE), BF)
        va[h, 0:HD, :] = local_ref[2, :, cols].astype(F32).T.astype(BF)
        va[h, HD : HD + 16, :] = jnp.ones((16, ROWS), BF)
    lpart[...] = jnp.zeros_like(lpart)

    @pl.when(z == 0)
    def _():
        zo_recv[0] = jnp.zeros((NZ, SHARE, HD), BF)
        zl_recv[0] = jnp.full((NZ, 8, HD), NONE, F32)

    @pl.when(z == NZ - 1)
    def _():
        zo_recv[1] = jnp.zeros((NZ, SHARE, HD), BF)
        zl_recv[1] = jnp.full((NZ, 8, HD), NONE, F32)

    def attend(column, half):
        def head(h, carry):
            cols = pl.ds(pl.multiple_of(h * HD, HD), HD)
            q = qbuf[column, pl.ds(4 * half, 4), :, cols].reshape(PACK, HD)
            nt = (((1,), (1,)), ((), ()))
            sc = lax.dot_general(win_ref[0, :, cols], q, nt, preferred_element_type=F32)
            sa = lax.dot_general(local_ref[1, :, cols], q, nt, preferred_element_type=F32)
            bias = bias_ref[pl.ds(h, 1), :]
            top = jnp.maximum(
                jnp.max(sc, axis=0, keepdims=True) * COEF - bias,
                jnp.max(sa, axis=0, keepdims=True) * COEF,
            )
            pc = jnp.exp2(sc * COEF - (top + bias)).astype(BF)
            pa = jnp.exp2(sa * COEF - top).astype(BF)
            acc = jnp.dot(vt[h], pc, preferred_element_type=F32) + jnp.dot(
                va[h], pa, preferred_element_type=F32
            )
            total = acc[HD : HD + 1]
            opart[column * 2 + half, cols, :] = (acc[:HD] * (1.0 / total)).astype(BF)
            lpart[column, pl.ds(half * 4 + h, 1), :] = top + jnp.log2(total)
            return carry

        lax.fori_loop(0, HEADS, head, 0)

    def arrivals(which, half):
        @pl.when(which == 1)
        def _():
            for j in (0, 2):
                y_wait(4 * half + j, 1)

        @pl.when(which == 2)
        def _():
            for j in (1, 3):
                y_wait(4 * half + j, 0)

        @pl.when(which == 3)
        def _():
            for j in range(4):
                y2_wait(4 * half + j)

    def pass_on(block):
        odd = block % 2

        @pl.when(odd == 0)
        def _():
            y_wait(block, 0)

        @pl.when(odd == 1)
        def _():
            y_wait(block, 1)

        y2_copy(block, odd).start()

    def gather_step(t, carry):
        @pl.when(jnp.logical_and(t >= 1, t < NZ))
        def _():
            @pl.when(z - t >= 0)
            def _():
                z_wait(z - t)

                @pl.when(z < NZ - 1)
                def _():
                    z_copy(z - t, 0).start()

                spread(z - t)

            @pl.when(z + t < NZ)
            def _():
                z_wait(z + t)

                @pl.when(z > 0)
                def _():
                    z_copy(z + t, 1).start()

                spread(z + t)

        @pl.when(jnp.logical_and(t >= 1, t <= NZ))
        def _():
            @pl.when(z - (t - 1) >= 0)
            def _():
                pass_on(z - (t - 1))

            @pl.when(jnp.logical_and(t > 1, z + (t - 1) < NZ))
            def _():
                pass_on(z + (t - 1))

        @pl.when(t == NZ)
        def _():
            for half in range(2):
                @pl.when(z // 2 + 4 * half != z)
                def _():
                    evict_z(half).start()

            @pl.when(jnp.logical_or(z == 0, z == NZ - 1))
            def _():
                evict_own().start()

        @pl.when(t >= 4)
        def _():
            b = t - 4
            half = jnp.where(b < 4, near, far)
            which = b % 4
            column = (y + which + jnp.where(which == 2, 1, 0) - jnp.where(which == 3, 1, 0)) % NY
            arrivals(which, half)
            attend(column, half)

        return carry

    lax.fori_loop(0, NZ + 4, gather_step, 0)

    def lse_copy(i):
        src, dev = ((yp, yp), (ym, ym), (y2, y2), (y2, yp), (y2, ym))[i]
        return copy(lpart.at[src], lrecv.at[i], ls_sem.at[i], lr_sem.at[i], at(z, dev))

    for i in range(5):
        lse_copy(i).start()

    def unit(u):
        half = jnp.where(u < 3, far, near)
        h = u % 3
        odd = u % 2
        cols = pl.ds(pl.multiple_of(h * HD, HD), HD)
        return half, h, odd, cols

    def raw1(u):
        half, h, odd, cols = unit(u)
        return copy(
            opart.at[y2 * 2 + half, cols, :], r1.at[u], r1s.at[u], r1r.at[u],
            at(z, yp + odd * (ym - yp)),
        )

    def raw2(u):
        half, h, odd, cols = unit(u)
        column = ym + odd * (yp - ym)
        return copy(
            opart.at[column * 2 + half, cols, :], r2.at[u], r2s.at[u], r2r.at[u], at(z, column)
        )

    def fwd(u):
        odd = u % 2
        return copy(
            relayed.at[u], r3.at[u], r3s.at[u], r3r.at[u], at(z, yp + odd * (ym - yp))
        )

    for u in range(2):
        raw1(u).start()
        raw2(u).start()

    for i in range(5):
        lse_copy(i).wait_recv()
    for side, column in ((0, yp), (1, ym)):
        got, own = lrecv[3 + side], lpart[column]
        both = lse2(got, own)
        wrelay[side, 0] = jnp.exp2(got - both)
        wrelay[side, 1] = jnp.exp2(own - both)
    own = lpart[y]
    everything = lse2(lrecv[0], lrecv[1], lrecv[2], own)
    w_m, w_p, w_2 = (jnp.exp2(lrecv[i] - everything) for i in range(3))
    wfinal[0, 0] = jnp.exp2(own - everything)
    wfinal[0, 1] = w_m + w_2
    wfinal[0, 2] = w_p
    wfinal[1, 0] = jnp.exp2(own - everything)
    wfinal[1, 1] = w_p + w_2
    wfinal[1, 2] = w_m
    for j in range(4):
        shifted = everything if j == 0 else pltpu.roll(everything, PACK - ROWS * j, 1)
        zl_own[j] = shifted[:, :HD]

    def relay(u):
        half, h, odd, cols = unit(u)
        row = pl.ds(half * 4 + h, 1)
        raw1(u).wait_recv()
        column = yp + odd * (ym - yp)
        mixed = r1[u].astype(F32) * wrelay[odd, 0, row, :] + opart[
            column * 2 + half, cols, :
        ].astype(F32) * wrelay[odd, 1, row, :]
        relayed[u] = mixed.astype(BF)
        fwd(u).start()

    def final(u):
        half, h, odd, cols = unit(u)
        row = pl.ds(half * 4 + h, 1)
        raw2(u).wait_recv()
        fwd(u).wait_recv()
        mixed = (
            opart[y * 2 + half, cols, :].astype(F32) * wfinal[odd, 0, row, :]
            + r3[u].astype(F32) * wfinal[odd, 1, row, :]
            + r2[u].astype(F32) * wfinal[odd, 2, row, :]
        )
        for j in range(4):
            shifted = mixed if j == 0 else pltpu.roll(mixed, PACK - ROWS * j, 1)
            zo_own[4 * half + j, cols, :] = shifted[:, :HD]

    def zo_copy(block, h, side):
        cols = pl.ds(pl.multiple_of(h * HD, HD), HD)
        return copy(
            zo_out.at[block, cols, :], zo_recv.at[side, block, cols, :], zos.at[block, h],
            zor.at[side, block, h], at(z + 1 - 2 * side, y),
        )

    def zl_copy(block, side):
        return copy(
            zl_out.at[block], zl_recv.at[side, block], zls.at[block], zlr.at[side, block],
            at(z + 1 - 2 * side, y),
        )

    def zo_wait(block, h, side):
        cols = pl.ds(pl.multiple_of(h * HD, HD), HD)
        copy(
            zo_out.at[block, cols, :], zo_recv.at[side, block, cols, :], zos.at[block, h],
            zor.at[side, block, h], at(z, yp),
        ).wait_recv()

    def zl_wait(block, side):
        copy(
            zl_out.at[block], zl_recv.at[side, block], zls.at[block], zlr.at[side, block],
            at(z, yp),
        ).wait_recv()

    def along(block, j, half, h, side):
        inner = z > 0 if side == 0 else z < NZ - 1

        @pl.when(h == 0)
        def _():
            @pl.when(inner)
            def _():
                zl_wait(block, side)

            got, own = zl_recv[side, block], zl_own[j]
            both = lse2(got, own)
            zl_out[block] = both
            zl_copy(block, side).start()
            wz[block, 0] = jnp.exp2(got - both)
            wz[block, 1] = jnp.exp2(own - both)

        @pl.when(inner)
        def _():
            zo_wait(block, h, side)

        cols = pl.ds(pl.multiple_of(h * HD, HD), HD)
        row = pl.ds(half * 4 + h, 1)
        mixed = (
            zo_recv[side, block, cols, :].astype(F32) * wz[block, 0, row, :]
            + zo_own[block, cols, :] * wz[block, 1, row, :]
        )
        zo_out[block, cols, :] = mixed.astype(BF)
        zo_copy(block, h, side).start()

    def z_phase(half, h):
        for j in (3, 0, 2, 1):
            block = 4 * half + j

            @pl.when(block > z)
            def _():
                along(block, j, half, h, 0)

            @pl.when(block < z)
            def _():
                along(block, j, half, h, 1)

    place = z + near * (NZ - 1 - 2 * z)

    def reduce_step(u, carry):
        @pl.when(u + 2 < 6)
        def _():
            raw1(u + 2).start()
            raw2(u + 2).start()

        @pl.when(u < 6)
        def _():
            relay(u)

        @pl.when(jnp.logical_and(u >= 1, u <= 6))
        def _():
            final(u - 1)

        uz = u - 1 - place

        @pl.when(jnp.logical_and(uz >= 0, uz < 3))
        def _():
            z_phase(far, uz)

        @pl.when(u == 5)
        def _():
            for which in range(2):
                @pl.when(2 * (z % 4) + which != z)
                def _():
                    rows = evict_rows(which, y)
                    copy(rows, rows, ezs.at[0], ezr.at[which], at(z, yp)).wait_recv()

            @pl.when(jnp.logical_or(z == 0, z == NZ - 1))
            def _():
                evict_own().wait()

            for which in range(2):
                evict_y(which, 0).start()
                evict_y(which, 1).start()

        @pl.when(u >= 5)
        def _():
            z_phase(near, u - 5)

        return carry

    lax.fori_loop(0, 8, reduce_step, 0)

    evict_y_wait(0, 0)
    evict_y2(0).start()
    evict_y_wait(1, 1)
    evict_y2(1).start()

    j = z % 4

    @pl.when(z > 0)
    def _():
        zl_wait(z, 0)

    @pl.when(z < NZ - 1)
    def _():
        zl_wait(z, 1)

    first, second, own = zl_recv[0, z], zl_recv[1, z], zl_own[j]
    total = lse2(first, second, own)
    wz[z, 0] = jnp.exp2(first - total)
    wz[z, 1] = jnp.exp2(second - total)
    wz[z, 2] = jnp.exp2(own - total)
    for h in range(HEADS):
        cols = pl.ds(h * HD, HD)
        row = pl.ds(near * 4 + h, 1)

        @pl.when(z > 0)
        def _():
            zo_wait(z, h, 0)

        @pl.when(z < NZ - 1)
        def _():
            zo_wait(z, h, 1)

        mixed = (
            zo_recv[0, z, cols, :].astype(F32) * wz[z, 0, row, :]
            + zo_recv[1, z, cols, :].astype(F32) * wz[z, 1, row, :]
            + zo_own[z, cols, :] * wz[z, 2, row, :]
        )
        out_ref[:, h * HD : (h + 1) * HD] = mixed.T[:ROWS].astype(BF)

    evict_y_wait(1, 0)
    evict_y_wait(0, 1)
    evict_y2_wait(0)
    evict_y2_wait(1)

    def drain(block, carry):
        @pl.when(jnp.logical_and(block <= z, z < NZ - 1))
        def _():
            z_copy(block, 0).wait_send()

        @pl.when(jnp.logical_and(block >= z, z > 0))
        def _():
            z_copy(block, 1).wait_send()

        y_copy(block, 0).wait_send()
        y_copy(block, 1).wait_send()
        y2_copy(block, block % 2).wait_send()

        @pl.when(block != z)
        def _():
            side = jnp.where(block > z, 0, 1)
            zl_copy(block, side).wait_send()
            for h in range(HEADS):
                zo_copy(block, h, side).wait_send()

        return carry

    lax.fori_loop(0, NZ, drain, 0)

    def drain_units(u, carry):
        raw1(u).wait_send()
        raw2(u).wait_send()
        fwd(u).wait_send()
        return carry

    lax.fori_loop(0, 6, drain_units, 0)
    for i in range(5):
        lse_copy(i).wait_send()
    for half in range(2):
        @pl.when(z // 2 + 4 * half != z)
        def _():
            evict_z(half).wait_send()
    for which in range(2):
        evict_y(which, 0).wait_send()
        evict_y(which, 1).wait_send()
        evict_y2(which).wait_send()


def attention(local, window, bias):
    dma = pltpu.SemaphoreType.DMA
    vm = pltpu.VMEM
    return pl.pallas_call(
        kernel,
        out_shape=(
            jax.ShapeDtypeStruct((ROWS, SHARE), BF),
            jax.ShapeDtypeStruct((2, CACHE, SHARE), BF),
        ),
        in_specs=[pl.BlockSpec(memory_space=pltpu.VMEM)] * 3,
        out_specs=(
            pl.BlockSpec(memory_space=pltpu.VMEM),
            pl.BlockSpec(memory_space=pl.ANY),
        ),
        scratch_shapes=[
            vm((NY, NZ, ROWS, SHARE), BF),
            vm((HEADS, HD + 16, CACHE), BF),
            vm((HEADS, HD + 16, ROWS), BF),
            vm((2 * NY, SHARE, PACK), BF),
            vm((NY, 8, PACK), F32),
            vm((5, 8, PACK), F32),
            vm((2, 2, 8, PACK), F32),
            vm((2, 3, 8, PACK), F32),
            vm((4, 8, HD), F32),
            vm((6, HD, PACK), BF),
            vm((6, HD, PACK), BF),
            vm((6, HD, PACK), BF),
            vm((6, HD, PACK), BF),
            vm((NZ, SHARE, HD), F32),
            vm((2, NZ, SHARE, HD), BF),
            vm((NZ, SHARE, HD), BF),
            vm((2, NZ, 8, HD), F32),
            vm((NZ, 8, HD), F32),
            vm((NZ, 3, 8, HD), F32),
            dma((2, NZ)), dma((NZ,)), dma((2, NZ)), dma((2, NZ)), dma((NZ,)), dma((NZ,)),
            dma((5,)), dma((5,)), dma((6,)), dma((6,)), dma((6,)), dma((6,)), dma((6,)), dma((6,)),
            dma((NZ, HEADS)), dma((2, NZ, HEADS)), dma((NZ,)), dma((2, NZ)),
            dma((2,)), dma((2,)), dma((2, 2)), dma((2, 2)), dma((2,)), dma((2,)), dma(()),
        ],
        compiler_params=pltpu.CompilerParams(
            collective_id=0, has_side_effects=True, vmem_limit_bytes=48 * 1024 * 1024
        ),
        cost_estimate=pl.CostEstimate(
            flops=4 * 3072 * 864 * SHARE, bytes_accessed=4 * 2**20, transcendentals=3072 * 864 * 3
        ),
    )(local, window, bias)


def body(active_qkv, window_kv, slot_owner, oldest_slot, timestep, time_slopes, gate_table):
    tok_dev = active_qkv.shape[1]
    ways = lax.axis_size("sp")
    groups = lax.axis_size("grp")
    split = active_qkv.reshape(3, tok_dev, ways, SHARE)
    local = lax.all_to_all(split, "sp", split_axis=2, concat_axis=1, tiled=True).reshape(
        3, ROWS, SHARE
    )
    group = lax.axis_index("grp")
    oldest = oldest_slot[0]
    group_ids = jnp.arange(groups, dtype=jnp.int32)
    my_slot = jnp.sum(jnp.where(group_ids == group, slot_owner, 0))
    age = (WIN - jnp.mod(my_slot - oldest, WIN)).astype(F32)
    slopes = lax.dynamic_slice_in_dim(time_slopes, lax.axis_index("sp") * HEADS, HEADS)
    bias = jnp.pad(slopes * (age * LOG2E), (0, 8 - HEADS))
    combined, moved = attention(local, window_kv, jnp.broadcast_to(bias[:, None], (8, PACK)))
    new_window = jnp.where(my_slot == oldest, moved, window_kv)
    returned = lax.all_to_all(combined, "sp", split_axis=0, concat_axis=1, tiled=True)
    gate = lax.dynamic_slice_in_dim(gate_table, timestep[0], 1, 0)
    attended = (gate * returned.astype(F32)).astype(BF)
    return (attended, new_window)


def solution(mesh):
    in_specs = (P(None, ("grp", "sp"), None), P(None, "grp", "sp"), P(), P(), P(), P(), P())
    out_specs = (P(("grp", "sp"), None), P(None, "grp", "sp"))
    return jax.shard_map(body, mesh=mesh, in_specs=in_specs, out_specs=out_specs, check_vma=False)
```

```python
import functools
import math

import jax
import jax.numpy as jnp
from jax import lax
from jax.experimental import pallas as pl
from jax.experimental.pallas import tpu as pltpu
from jax.sharding import PartitionSpec as P

HD = 128
WIN = 8
HEADS = 3
SHARE = HEADS * HD
TOK = 6
ROWS = 96
HALF = 48
CACHE = 768
NZ = 8
NY = 4
NXC = 8
PACK = 4 * ROWS
OUT1 = 112
BACK1 = 48
SUMS = HD + 16
LOG2E = math.log2(math.e)
COEF = LOG2E / math.sqrt(HD)
NONE = -1e30
MESH = pl.DeviceIdType.MESH
BF = jnp.bfloat16
F32 = jnp.float32
NT = (((1,), (1,)), ((), ()))


def lse2(*parts):
    top = functools.reduce(jnp.maximum, parts)
    return top + jnp.log2(sum(jnp.exp2(p - top) for p in parts))


def kernel(
    x_ref, win_ref, owner_ref, oldest_ref, slope_ref, out_ref, moved_ref,
    pack32, packb, recv1, dense, local, qbuf, kbuf, vt, akv, vta, acc_ref,
    zo_own, zo_recv, zo_out, zl_own, zl_recv, zl_out, comb, back, ret, recv2,
    s1s, s1r, s2s, s2r, zsend, zrecv, ks, kr, vs, vr, acs, acr,
    zos, zor, zls, zlr, ezs, ezr, eys, eyr, cs, cr, ds, dr, cp_sem,
):
    me = lax.axis_index("grp")
    sp = lax.axis_index("sp")
    z = me // NY
    y = me % NY
    zh = sp // NXC
    xc = sp % NXC
    near = z // 4
    far = 1 - near

    def at(zz, yy):
        return {"grp": zz * NY + yy, "sp": sp}

    def beside(other):
        return {"grp": me, "sp": zh * NXC + other}

    across = {"grp": me, "sp": (1 - zh) * NXC + xc}

    def copy(src, dst, send, recv, dev):
        return pltpu.make_async_remote_copy(
            src_ref=src, dst_ref=dst, send_sem=send, recv_sem=recv,
            device_id=dev, device_id_type=MESH,
        )

    def head_cols(h):
        return pl.ds(pl.multiple_of(h * HD, HD), HD)

    barrier = pltpu.get_barrier_semaphore()
    peers = [at((z + i) % NZ, y) for i in range(1, NZ)]
    peers += [at(z, (y + i) % NY) for i in range(1, NY)]
    peers += [beside((xc + i) % NXC) for i in range(1, NXC)]
    peers += [across]
    for peer in peers:
        pl.semaphore_signal(barrier, inc=1, device_id=peer, device_id_type=MESH)
    pl.semaphore_wait(barrier, len(peers))

    def k_copy(h, i):
        return copy(
            win_ref.at[0, :, h * HD : (h + 1) * HD], kbuf.at[y, h], ks.at[i, h], kr.at[i, h],
            at(z, (y + i) % NY),
        )

    def v_copy(h, i):
        return copy(
            vt.at[y, h, pl.ds(0, HD), :], vt.at[y, h, pl.ds(0, HD), :], vs.at[i, h], vr.at[i, h],
            at(z, (y + i) % NY),
        )

    def kv_wait(h, i):
        src = (y + NY - i) % NY
        copy(kbuf.at[src, h], kbuf.at[src, h], ks.at[i, h], kr.at[i, h], at(z, src)).wait_recv()
        rows = vt.at[src, h, pl.ds(0, HD), :]
        copy(rows, rows, vs.at[i, h], vr.at[i, h], at(z, src)).wait_recv()

    for i in (1, 3, 2):
        k_copy(0, i).start()

    def step1(other):
        return copy(packb.at[other], recv1.at[xc], s1s.at[other], s1r.at[xc], beside(other))

    def step1_wait(other):
        copy(recv1.at[other], recv1.at[other], s1s.at[other], s1r.at[other], beside(other)).wait_recv()

    def piece(half, t, h):
        return half * 54 + (t * HEADS + h) * TOK

    for d in range(NXC):
        for half in range(2):
            for t in range(3):
                for h in range(HEADS):
                    col = ((half * NXC + d) * HEADS + h) * HD
                    row = piece(half, t, h)
                    pack32[d, row : row + TOK, :] = x_ref[t, :, col : col + HD].astype(F32)
        packb[d] = pack32[d].astype(BF)
    for i in range(1, NXC):
        step1((xc + i) % NXC).start()
    recv1[xc] = packb[xc]

    for h in range(HEADS):
        vt[y, h, 0:HD, :] = win_ref[1, :, h * HD : (h + 1) * HD].astype(F32).T.astype(BF)
        if h < 2:
            for i in (1, 3, 2):
                v_copy(h, i).start()
        if h == 0:
            for i in (1, 3, 2):
                k_copy(1, i).start()
        kbuf[y, h] = win_ref[0, :, h * HD : (h + 1) * HD]
        for src in range(NY):
            vt[src, h, HD:SUMS, :] = jnp.ones((SUMS - HD, CACHE), BF)
        vta[h, HD:SUMS, :] = jnp.ones((SUMS - HD, PACK), BF)

    @pl.when(z == 0)
    def _():
        zo_recv[0] = jnp.zeros((NZ, SHARE, HD), BF)
        zl_recv[0] = jnp.full((NZ, HEADS, 8, HD), NONE, F32)

    @pl.when(z == NZ - 1)
    def _():
        zo_recv[1] = jnp.zeros((NZ, SHARE, HD), BF)
        zl_recv[1] = jnp.full((NZ, HEADS, 8, HD), NONE, F32)

    for i in range(1, NXC):
        step1_wait((xc + i) % NXC)
    for s in range(NXC):
        pack32[s] = recv1[s].astype(F32)
    for t in range(3):
        for s in range(NXC):
            for half in range(2):
                for h in range(HEADS):
                    row = piece(half, t, h)
                    dense[half, t, s * TOK : (s + 1) * TOK, h * HD : (h + 1) * HD] = pack32[
                        s, row : row + TOK, :
                    ]

    mine = pl.ds(pl.multiple_of(zh * HALF, HALF), HALF)
    theirs = pl.ds(pl.multiple_of((1 - zh) * HALF, HALF), HALF)

    def step2(t, n):
        part = back.at[pl.ds(t, n)]
        return copy(part, local.at[pl.ds(t, n), mine, :], s2s.at[t], s2r.at[t], across)

    def step2_wait(t, n):
        part = local.at[pl.ds(t, n), theirs, :]
        copy(part, part, s2s.at[t], s2r.at[t], across).wait_recv()

    back[0] = dense[1 - zh, 0].astype(BF)
    step2(0, 1).start()
    for t in (1, 2):
        back[t] = dense[1 - zh, t].astype(BF)
    step2(1, 2).start()
    for t in range(3):
        local[t, mine, :] = dense[zh, t].astype(BF)

    def z_copy(block, h, side):
        part = qbuf.at[block, :, head_cols(h)]
        return copy(
            part, part, zsend.at[side, block, h], zrecv.at[block, h], at(z + 1 - 2 * side, y)
        )

    def z_wait(block, h):
        part = qbuf.at[block, :, head_cols(h)]
        copy(part, part, zsend.at[0, block, h], zrecv.at[block, h], across).wait_recv()

    step2_wait(0, 1)
    qbuf[z] = local[0]
    for h in range(HEADS):
        @pl.when(z < NZ - 1)
        def _():
            z_copy(z, h, 0).start()

        @pl.when(z > 0)
        def _():
            z_copy(z, h, 1).start()

    def gather_step(t):
        for h in range(HEADS):
            @pl.when(z - t >= 0)
            def _():
                z_wait(z - t, h)

                @pl.when(z < NZ - 1)
                def _():
                    z_copy(z - t, h, 0).start()

            @pl.when(z + t < NZ)
            def _():
                z_wait(z + t, h)

                @pl.when(z > 0)
                def _():
                    z_copy(z + t, h, 1).start()

    def a_copy(i):
        return copy(akv.at[y], akv.at[y], acs.at[i], acr.at[i], at(z, (y + i) % NY))

    def a_wait(i):
        src = (y + NY - i) % NY
        copy(akv.at[src], akv.at[src], acs.at[i], acr.at[i], at(z, src)).wait_recv()

    def evict_rows(which, column):
        return moved_ref.at[:, pl.ds((which * NY + column) * ROWS, ROWS), :]

    def evict_z(half):
        return copy(
            akv.at[y], evict_rows(z % 2, y), ezs.at[half], ezr.at[z % 2], at(z // 2 + 4 * half, y)
        )

    def evict_own():
        return pltpu.make_async_copy(akv.at[y], evict_rows(z % 2, y), cp_sem)

    def evict_y(which, i):
        rows = evict_rows(which, y)
        return copy(rows, rows, eys.at[which, i], eyr.at[which, i], at(z, (y + i) % NY))

    def evict_y_wait(which, i):
        src = (y + NY - i) % NY
        rows = evict_rows(which, src)
        copy(rows, rows, eys.at[which, i], eyr.at[which, i], at(z, src)).wait_recv()

    def attend(h, half):
        cols = head_cols(h)
        q = qbuf[pl.ds(4 * half, 4), :, cols].reshape(PACK, HD)
        slope = slope_ref[sp * HEADS + h] * LOG2E

        sa = lax.dot_general(
            akv[:, 0, :, cols].reshape(PACK, HD), q, NT, preferred_element_type=F32
        )
        first = jnp.max(sa, axis=0, keepdims=True) * COEF
        pa = jnp.exp2(sa * COEF - first).astype(BF)
        acc_ref[...] = jnp.dot(vta[h], pa, preferred_element_type=F32)

        def chunk(src, top):
            slot = owner_ref[z * NY + src] - oldest_ref[0]
            age = WIN - (slot + WIN) % WIN
            bias = slope * age.astype(F32)
            s = lax.dot_general(kbuf[src, h], q, NT, preferred_element_type=F32)
            new = jnp.maximum(top, jnp.max(s, axis=0, keepdims=True) * COEF - bias)
            p = jnp.exp2(s * COEF - (new + bias)).astype(BF)
            acc_ref[...] = acc_ref[...] * jnp.exp2(top - new) + jnp.dot(
                vt[src, h], p, preferred_element_type=F32
            )
            return new

        top = lax.fori_loop(0, NY, chunk, first)
        total = acc_ref[HD : HD + 1, :]
        mixed = acc_ref[0:HD, :] * (1.0 / total)
        lse = jnp.broadcast_to(top + jnp.log2(total), (8, PACK))
        for j in range(4):
            back_by = PACK - ROWS * j
            part = mixed if j == 0 else pltpu.roll(mixed, back_by, 1)
            zo_own[4 * half + j, cols, :] = part[:, :HD]
            part = lse if j == 0 else pltpu.roll(lse, back_by, 1)
            zl_own[4 * half + j, h] = part[:, :HD]

    def zo_copy(block, h, side, dev):
        cols = head_cols(h)
        return copy(
            zo_out.at[block, cols, :], zo_recv.at[side, block, cols, :], zos.at[block, h],
            zor.at[side, block, h], dev,
        )

    def zl_copy(block, h, side, dev):
        return copy(
            zl_out.at[block, h], zl_recv.at[side, block, h], zls.at[block, h],
            zlr.at[side, block, h], dev,
        )

    def along(block, h, side):
        inner = z > 0 if side == 0 else z < NZ - 1
        onward = at(z + 1 - 2 * side, y)
        cols = head_cols(h)

        @pl.when(inner)
        def _():
            zl_copy(block, h, side, across).wait_recv()
            zo_copy(block, h, side, across).wait_recv()

        got, own = zl_recv[side, block, h], zl_own[block, h]
        both = lse2(got, own)
        zl_out[block, h] = both
        mixed = (
            zo_recv[side, block, cols, :].astype(F32) * jnp.exp2(got - both)[0:1]
            + zo_own[block, cols, :] * jnp.exp2(own - both)[0:1]
        )
        zo_out[block, cols, :] = mixed.astype(BF)
        zl_copy(block, h, side, onward).start()
        zo_copy(block, h, side, onward).start()

    def upward(h, half):
        for j in (3, 2, 1, 0):
            @pl.when(4 * half + j > z)
            def _():
                along(4 * half + j, h, 0)

    def downward(h, half):
        for j in range(4):
            @pl.when(4 * half + j < z)
            def _():
                along(4 * half + j, h, 1)

    def tick(e, carry):
        @pl.when(e < NZ)
        def _():
            gather_step(e)

        @pl.when(e == 2)
        def _():
            step2_wait(1, 2)
            akv[y] = local[1:3]
            for i in (1, 3, 2):
                a_copy(i).start()
            for i in (1, 3, 2):
                k_copy(2, i).start()
                v_copy(2, i).start()

        @pl.when(e == NZ - 1)
        def _():
            for half in range(2):
                @pl.when(z // 2 + 4 * half != z)
                def _():
                    evict_z(half).start()

            @pl.when(jnp.logical_or(z == 0, z == NZ - 1))
            def _():
                evict_own().start()

        @pl.when(e == 6)
        def _():
            for i in (1, 3, 2):
                a_wait(i)
            for h in range(HEADS):
                values = akv[:, 1, :, h * HD : (h + 1) * HD].reshape(PACK, HD)
                vta[h, 0:HD, :] = values.astype(F32).T.astype(BF)

        for h, first in ((0, 6), (1, 9), (2, 11)):
            @pl.when(e == first)
            def _():
                for i in (1, 3, 2):
                    kv_wait(h, i)

        @pl.when(jnp.logical_or(e == 6, jnp.logical_and(e >= 8, e <= 12)))
        def _():
            h = jnp.where(e >= 11, 2, jnp.where(e >= 9, 1, 0))
            is_near = jnp.logical_or(e == 6, jnp.logical_or(e == 10, e == 12))
            attend(h, jnp.where(is_near, near, far))

        def sums(h, carry):
            far_at = 8 + h + h // 2
            near_at = 8 + 2 * h

            @pl.when(e == far_at + z)
            def _():
                upward(h, 1)

            @pl.when(e == far_at + NZ - 1 - z)
            def _():
                downward(h, 0)

            @pl.when(jnp.logical_and(z < 3, e == near_at + z))
            def _():
                upward(h, 0)

            @pl.when(jnp.logical_and(z > 4, e == near_at + NZ - 1 - z))
            def _():
                downward(h, 1)

            return carry

        @pl.when(e >= 8)
        def _():
            lax.fori_loop(0, HEADS, sums, 0)

        @pl.when(e == 13)
        def _():
            for which in range(2):
                @pl.when(2 * (z % 4) + which != z)
                def _():
                    rows = evict_rows(which, y)
                    copy(rows, rows, ezs.at[0], ezr.at[which], across).wait_recv()

            @pl.when(jnp.logical_or(z == 0, z == NZ - 1))
            def _():
                evict_own().wait()

            for which in range(2):
                for i in (1, 3, 2):
                    evict_y(which, i).start()

        return carry

    lax.fori_loop(1, 19, tick, 0)

    for h in range(HEADS):
        cols = head_cols(h)
        for side, inner in ((0, z > 0), (1, z < NZ - 1)):
            @pl.when(inner)
            def _():
                zl_copy(z, h, side, across).wait_recv()
                zo_copy(z, h, side, across).wait_recv()

        first, second, own = zl_recv[0, z, h], zl_recv[1, z, h], zl_own[z, h]
        whole = lse2(first, second, own)
        mixed = (
            zo_recv[0, z, cols, :].astype(F32) * jnp.exp2(first - whole)[0:1]
            + zo_recv[1, z, cols, :].astype(F32) * jnp.exp2(second - whole)[0:1]
            + zo_own[z, cols, :] * jnp.exp2(own - whole)[0:1]
        )
        comb[:, h * HD : (h + 1) * HD] = mixed.T[:ROWS].astype(BF)

    def return2(dev):
        return copy(comb.at[theirs, :], ret.at[zh], cs, cr, dev)

    return2(across).start()
    ret[zh] = comb[mine, :]
    part = ret.at[1 - zh]
    copy(part, part, cs, cr, across).wait_recv()
    dense[0, 0] = ret[0].astype(F32)
    dense[1, 0] = ret[1].astype(F32)

    def return1(other):
        return copy(
            packb.at[other, pl.ds(0, BACK1), :], recv2.at[xc], ds.at[other], dr.at[xc],
            beside(other),
        )

    def return1_wait(other):
        part = recv2.at[other]
        copy(part, part, ds.at[other], dr.at[other], beside(other)).wait_recv()

    for i in range(1, NXC):
        step1((xc + i) % NXC).wait_send()
    for d in range(NXC):
        for half in range(2):
            for h in range(HEADS):
                row = (half * HEADS + h) * TOK
                pack32[d, row : row + TOK, :] = dense[
                    half, 0, d * TOK : (d + 1) * TOK, h * HD : (h + 1) * HD
                ]
        packb[d, 0:BACK1, :] = pack32[d, 0:BACK1, :].astype(BF)
    for i in range(1, NXC):
        return1((xc + i) % NXC).start()
    recv2[xc] = packb[xc, 0:BACK1, :]
    for i in range(1, NXC):
        return1_wait((xc + i) % NXC)
    for s in range(NXC):
        pack32[s, 0:BACK1, :] = recv2[s].astype(F32)
        for half in range(2):
            for h in range(HEADS):
                row = (half * HEADS + h) * TOK
                col = ((half * NXC + s) * HEADS + h) * HD
                out_ref[:, col : col + HD] = pack32[s, row : row + TOK, :]

    for which in range(2):
        for i in (1, 3, 2):
            evict_y_wait(which, i)
    return2(across).wait_send()
    step2(0, 1).wait_send()
    step2(1, 2).wait_send()
    for i in range(1, NXC):
        return1((xc + i) % NXC).wait_send()
    for i in (1, 2, 3):
        a_copy(i).wait_send()
        for which in range(2):
            evict_y(which, i).wait_send()
        for h in range(HEADS):
            k_copy(h, i).wait_send()
            v_copy(h, i).wait_send()
    for half in range(2):
        @pl.when(z // 2 + 4 * half != z)
        def _():
            evict_z(half).wait_send()

    def drain(block, carry):
        for h in range(HEADS):
            @pl.when(jnp.logical_and(block <= z, z < NZ - 1))
            def _():
                z_copy(block, h, 0).wait_send()

            @pl.when(jnp.logical_and(block >= z, z > 0))
            def _():
                z_copy(block, h, 1).wait_send()

            @pl.when(block != z)
            def _():
                zl_copy(block, h, 0, across).wait_send()
                zo_copy(block, h, 0, across).wait_send()

        return carry

    lax.fori_loop(0, NZ, drain, 0)


def attention(x, window, owner, oldest, slopes):
    dma = pltpu.SemaphoreType.DMA
    vm = pltpu.VMEM
    in_vmem = pl.BlockSpec(memory_space=pltpu.VMEM)
    in_smem = pl.BlockSpec(memory_space=pltpu.SMEM)
    return pl.pallas_call(
        kernel,
        out_shape=(
            jax.ShapeDtypeStruct((TOK, 2 * NXC * SHARE), F32),
            jax.ShapeDtypeStruct((2, CACHE, SHARE), BF),
        ),
        in_specs=[in_vmem, in_vmem, in_smem, in_smem, in_smem],
        out_specs=(in_vmem, pl.BlockSpec(memory_space=pl.ANY)),
        scratch_shapes=[
            vm((NXC, OUT1, HD), F32),
            vm((NXC, OUT1, HD), BF),
            vm((NXC, OUT1, HD), BF),
            vm((2, 3, HALF, SHARE), F32),
            vm((3, ROWS, SHARE), BF),
            vm((NZ, ROWS, SHARE), BF),
            vm((NY, HEADS, CACHE, HD), BF),
            vm((NY, HEADS, SUMS, CACHE), BF),
            vm((NY, 2, ROWS, SHARE), BF),
            vm((HEADS, SUMS, PACK), BF),
            vm((SUMS, PACK), F32),
            vm((NZ, SHARE, HD), F32),
            vm((2, NZ, SHARE, HD), BF),
            vm((NZ, SHARE, HD), BF),
            vm((NZ, HEADS, 8, HD), F32),
            vm((2, NZ, HEADS, 8, HD), F32),
            vm((NZ, HEADS, 8, HD), F32),
            vm((ROWS, SHARE), BF),
            vm((3, HALF, SHARE), BF),
            vm((2, HALF, SHARE), BF),
            vm((NXC, BACK1, HD), BF),
            dma((NXC,)), dma((NXC,)),
            dma((3,)), dma((3,)),
            dma((2, NZ, HEADS)), dma((NZ, HEADS)),
            dma((NY, HEADS)), dma((NY, HEADS)), dma((NY, HEADS)), dma((NY, HEADS)),
            dma((NY,)), dma((NY,)),
            dma((NZ, HEADS)), dma((2, NZ, HEADS)), dma((NZ, HEADS)), dma((2, NZ, HEADS)),
            dma((2,)), dma((2,)), dma((2, NY)), dma((2, NY)),
            dma(()), dma(()), dma((NXC,)), dma((NXC,)), dma(()),
        ],
        compiler_params=pltpu.CompilerParams(
            collective_id=0, has_side_effects=True, vmem_limit_bytes=48 * 1024 * 1024
        ),
        cost_estimate=pl.CostEstimate(
            flops=4 * 3072 * 864 * SHARE, bytes_accessed=4 * 2**20, transcendentals=3072 * 864 * 3
        ),
    )(x, window, owner, oldest, slopes)


def body(active_qkv, window_kv, slot_owner, oldest_slot, timestep, time_slopes, gate_table):
    combined, moved = attention(active_qkv, window_kv, slot_owner, oldest_slot, time_slopes)
    my_slot = lax.dynamic_slice_in_dim(slot_owner, lax.axis_index("grp"), 1, 0)[0]
    new_window = jnp.where(my_slot == oldest_slot[0], moved, window_kv)
    gate = lax.dynamic_slice_in_dim(gate_table, timestep[0], 1, 0)
    return ((gate * combined).astype(BF), new_window)


def solution(mesh):
    in_specs = (P(None, ("grp", "sp"), None), P(None, "grp", "sp"), P(), P(), P(), P(), P())
    out_specs = (P(("grp", "sp"), None), P(None, "grp", "sp"))
    return jax.shard_map(body, mesh=mesh, in_specs=in_specs, out_specs=out_specs, check_vma=False)
```

```python
import functools
import math

import jax
import jax.numpy as jnp
from jax import lax
from jax.experimental import pallas as pl
from jax.experimental.pallas import tpu as pltpu
from jax.sharding import PartitionSpec as P

HD = 128
WIN = 8
HEADS = 3
SHARE = HEADS * HD
TOK = 6
ROWS = 96
HALF = 48
CACHE = 768
NZ = 8
NY = 4
NXC = 8
PACK = 4 * ROWS
OUT1 = 112
BACK1 = 48
SUMS = HD + 16
LOG2E = math.log2(math.e)
COEF = LOG2E / math.sqrt(HD)
NONE = -1e30
MESH = pl.DeviceIdType.MESH
BF = jnp.bfloat16
F32 = jnp.float32
NT = (((1,), (1,)), ((), ()))


def lse2(*parts):
    top = functools.reduce(jnp.maximum, parts)
    return top + jnp.log2(sum(jnp.exp2(p - top) for p in parts))


def kernel(
    x_hbm, win_ref, owner_hbm, oldest_hbm, slope_hbm, out_ref, moved_ref, flag_ref,
    x_ref, vbuf, owner_ref, oldest_ref, slope_ref, in_sem,
    pack32, packb, recv1, dense, local, qbuf, kbuf, vt, akv, vta, acc_ref, top_ref,
    so, sl, qo, ql, mo, ml, fo, fl, back, recv2,
    s1s, s1r, s2s, s2r, zsend, zrecv, ks, kr, vs, vr, k2s, k2r, v2s, v2r, acs, acr, a2s, a2r,
    qos, qor, qls, qlr, fos, for_, fls, flr, ezs, ezr, eys, eyr, e2s, e2r, ds, dr, cp_sem,
):
    me = lax.axis_index("grp")
    sp = lax.axis_index("sp")
    z = me // NY
    y = me % NY
    zh = sp // NXC
    xc = sp % NXC
    quad = z // 4
    seat = z % 4

    def at(zz, yy):
        return {"grp": zz * NY + yy, "sp": sp}

    def beside(other):
        return {"grp": me, "sp": zh * NXC + other}

    across = {"grp": me, "sp": (1 - zh) * NXC + xc}
    over = (z + 4) % NZ
    across_over = {"grp": over * NY + y, "sp": (1 - zh) * NXC + xc}

    def copy(src, dst, send, recv, dev):
        return pltpu.make_async_remote_copy(
            src_ref=src, dst_ref=dst, send_sem=send, recv_sem=recv,
            device_id=dev, device_id_type=MESH,
        )

    def head_cols(h):
        return pl.ds(pl.multiple_of(h * HD, HD), HD)

    loads = [
        pltpu.make_async_copy(src, dst, in_sem.at[i])
        for i, (src, dst) in enumerate(
            [
                (x_hbm, x_ref), (win_ref.at[1], vbuf), (owner_hbm, owner_ref),
                (oldest_hbm, oldest_ref), (slope_hbm, slope_ref),
            ]
            + [(win_ref.at[0, :, h * HD : (h + 1) * HD], kbuf.at[y, h]) for h in range(HEADS)]
        )
    ]
    for load in loads:
        load.start()

    barrier = pltpu.get_barrier_semaphore()
    peers = [at((z + i) % NZ, y) for i in range(1, NZ)]
    peers += [at(z, (y + i) % NY) for i in range(1, NY)]
    peers += [beside((xc + i) % NXC) for i in range(1, NXC)]
    peers += [across, across_over]
    for peer in peers:
        pl.semaphore_signal(barrier, inc=1, device_id=peer, device_id_type=MESH)
    pl.semaphore_wait(barrier, len(peers))

    def k_copy(h, i):
        return copy(
            win_ref.at[0, :, h * HD : (h + 1) * HD], kbuf.at[y, h], ks.at[i, h], kr.at[i, h],
            at(z, (y + i) % NY),
        )

    def v_copy(h, i):
        return copy(
            vt.at[y, h, pl.ds(0, HD), :], vt.at[y, h, pl.ds(0, HD), :], vs.at[i, h], vr.at[i, h],
            at(z, (y + i) % NY),
        )

    def kv_wait(h, i):
        src = (y + NY - i) % NY
        copy(kbuf.at[src, h], kbuf.at[src, h], ks.at[i, h], kr.at[i, h], at(z, src)).wait_recv()
        rows = vt.at[src, h, pl.ds(0, HD), :]
        copy(rows, rows, vs.at[i, h], vr.at[i, h], at(z, src)).wait_recv()

    def halves(src, h, part):
        rows = pl.ds(part * PACK, PACK)
        return kbuf.at[src, h, rows, :], vt.at[src, h, pl.ds(0, HD), rows]

    def relay_copies(src, h, part):
        dev = at(z, (y + 1 + 2 * part) % NY)
        keys, values = halves(src, h, part)
        return (
            copy(keys, keys, k2s.at[part, h], k2r.at[part, h], dev),
            copy(values, values, v2s.at[part, h], v2r.at[part, h], dev),
        )

    def relay(h):
        for part, i in ((0, 1), (1, 3)):
            kv_wait(h, i)
            for each in relay_copies((y + NY - i) % NY, h, part):
                each.start()

    def relay_wait(h, part):
        for each in relay_copies((y + 2) % NY, h, part):
            each.wait_recv()

    for i in (1, 3):
        k_copy(0, i).start()

    def step1(other):
        return copy(packb.at[other], recv1.at[xc], s1s.at[other], s1r.at[xc], beside(other))

    def step1_wait(other):
        copy(recv1.at[other], recv1.at[other], s1s.at[other], s1r.at[other], beside(other)).wait_recv()

    def piece(half, t, h):
        return half * 54 + (t * HEADS + h) * TOK

    loads[0].wait()
    for d in range(NXC):
        for half in range(2):
            for t in range(3):
                for h in range(HEADS):
                    col = ((half * NXC + d) * HEADS + h) * HD
                    row = piece(half, t, h)
                    pack32[d, row : row + TOK, :] = x_ref[t, :, col : col + HD].astype(F32)
        packb[d] = pack32[d].astype(BF)
    for i in range(1, NXC):
        step1((xc + i) % NXC).start()
    recv1[xc] = packb[xc]

    loads[1].wait()
    for h in range(HEADS):
        vt[y, h, 0:HD, :] = vbuf[:, h * HD : (h + 1) * HD].astype(F32).T.astype(BF)
        if h < 2:
            for i in (1, 3):
                v_copy(h, i).start()
        if h == 0:
            for i in (1, 3):
                k_copy(1, i).start()
        for src in range(NY):
            vt[src, h, HD:SUMS, :] = jnp.ones((SUMS - HD, CACHE), BF)
        vta[h, HD:SUMS, :] = jnp.ones((SUMS - HD, PACK), BF)
    for load in loads[2:]:
        load.wait()
    flag_ref[...] = jnp.full((8, HD), (owner_ref[me] == oldest_ref[0]).astype(F32))

    theirs = pl.ds(pl.multiple_of((1 - zh) * HALF, HALF), HALF)
    for h in range(HEADS):
        for i in range(4):
            qo[h, i, :, ROWS:HD, :] = jnp.zeros((2, HD - ROWS, HD), BF)
        for half in range(2):
            fo[half, h, :, ROWS:HD, :] = jnp.zeros((2, HD - ROWS, HD), BF)
            fo[half, h, :, theirs, :] = jnp.zeros((2, HALF, HD), BF)

    for i in range(1, NXC):
        step1_wait((xc + i) % NXC)
    for s in range(NXC):
        pack32[s] = recv1[s].astype(F32)
    for t in range(3):
        for s in range(NXC):
            for half in range(2):
                for h in range(HEADS):
                    row = piece(half, t, h)
                    dense[half, t, s * TOK : (s + 1) * TOK, h * HD : (h + 1) * HD] = pack32[
                        s, row : row + TOK, :
                    ]

    mine = pl.ds(pl.multiple_of(zh * HALF, HALF), HALF)

    def step2(t, n):
        part = back.at[pl.ds(t, n)]
        return copy(part, local.at[pl.ds(t, n), mine, :], s2s.at[t], s2r.at[t], across)

    def step2_wait(t, n):
        part = local.at[pl.ds(t, n), theirs, :]
        copy(part, part, s2s.at[t], s2r.at[t], across).wait_recv()

    back[0] = dense[1 - zh, 0].astype(BF)
    step2(0, 1).start()
    for t in (1, 2):
        back[t] = dense[1 - zh, t].astype(BF)
    step2(1, 2).start()
    for t in range(3):
        local[t, mine, :] = dense[zh, t].astype(BF)

    def z_copy(block, h, side):
        part = qbuf.at[block, :, head_cols(h)]
        return copy(
            part, part, zsend.at[side, block, h], zrecv.at[block, h], at(z + 1 - 2 * side, y)
        )

    def z_wait(block, h):
        part = qbuf.at[block, :, head_cols(h)]
        copy(part, part, zsend.at[0, block, h], zrecv.at[block, h], across).wait_recv()

    step2_wait(0, 1)
    qbuf[z] = local[0]
    for h in range(HEADS):
        @pl.when(z < NZ - 1)
        def _():
            z_copy(z, h, 0).start()

        @pl.when(z > 0)
        def _():
            z_copy(z, h, 1).start()

    def gather_step(t):
        for h in range(HEADS):
            @pl.when(z - t >= 0)
            def _():
                z_wait(z - t, h)

                @pl.when(z < NZ - 1)
                def _():
                    z_copy(z - t, h, 0).start()

            @pl.when(z + t < NZ)
            def _():
                z_wait(z + t, h)

                @pl.when(z > 0)
                def _():
                    z_copy(z + t, h, 1).start()

    def a_copy(i):
        return copy(akv.at[y], akv.at[y], acs.at[i], acr.at[i], at(z, (y + i) % NY))

    def a_wait(i):
        src = (y + NY - i) % NY
        copy(akv.at[src], akv.at[src], acs.at[i], acr.at[i], at(z, src)).wait_recv()

    def a_relay(src, part):
        rows = akv.at[src, part]
        return copy(rows, rows, a2s.at[part], a2r.at[part], at(z, (y + 1 + 2 * part) % NY))

    def evict_rows(which, column):
        return moved_ref.at[:, pl.ds((which * NY + column) * ROWS, ROWS), :]

    def evict_z(half):
        return copy(
            akv.at[y], evict_rows(z % 2, y), ezs.at[half], ezr.at[z % 2], at(z // 2 + 4 * half, y)
        )

    def evict_own():
        return pltpu.make_async_copy(akv.at[y], evict_rows(z % 2, y), cp_sem)

    def evict_y(which, i):
        rows = evict_rows(which, y)
        return copy(rows, rows, eys.at[which, i], eyr.at[which, i], at(z, (y + i) % NY))

    def evict_relay(which, src):
        rows = evict_rows(which, src)
        return copy(rows, rows, e2s.at[which], e2r.at[which], at(z, (y + 1 + 2 * which) % NY))

    def evict_y_wait(which, i):
        src = (y + NY - i) % NY
        rows = evict_rows(which, src)
        copy(rows, rows, eys.at[which, i], eyr.at[which, i], at(z, src)).wait_recv()

    def attend(h, sources, start, stop):
        cols = head_cols(h)
        q = qbuf[:, :, cols].reshape(NZ * ROWS, HD)
        slope = slope_ref[sp * HEADS + h] * LOG2E

        def window(i, part):
            src = (y + NY - i) % NY
            rows = slice(part * PACK, (part + 1) * PACK)
            slot = owner_ref[z * NY + src] - oldest_ref[0]
            age = WIN - (slot + WIN) % WIN
            return kbuf[src, h, rows, :], vt.at[src, h, :, rows], slope * age.astype(F32)

        chunks = [(akv[:, 0, :, cols].reshape(PACK, HD), vta.at[h], None)] if start else []
        chunks += [window(i, part) for i in sources for part in range(2)]
        top, acc = (None, None) if start else (top_ref[0:1, :], acc_ref[...])
        ahead = lax.dot_general(chunks[0][0], q, NT, preferred_element_type=F32)
        for n, (_, values, bias) in enumerate(chunks):
            score = ahead
            if n + 1 < len(chunks):
                ahead = lax.dot_general(chunks[n + 1][0], q, NT, preferred_element_type=F32)
            new = jnp.max(score, axis=0, keepdims=True) * COEF
            if bias is not None:
                new = new - bias
            if top is not None:
                new = jnp.maximum(top, new)
            weight = jnp.exp2(score * COEF - (new if bias is None else new + bias))
            part = jnp.dot(values[...], weight.astype(BF), preferred_element_type=F32)
            acc = part if top is None else acc * jnp.exp2(top - new) + part
            top = new
        if not stop:
            top_ref[...] = jnp.broadcast_to(top, (8, NZ * ROWS))
            acc_ref[...] = acc
            return
        total = acc[HD : HD + 1]
        mixed = acc[:HD] * (1.0 / total)
        lse = jnp.broadcast_to(top + jnp.log2(total), (8, NZ * ROWS))
        for j in range(NZ):
            pack = slice(j // 4 * PACK, (j // 4 + 1) * PACK)
            tokens, sums = mixed[:, pack], lse[:, pack]
            if j % 4:
                tokens = pltpu.roll(tokens, PACK - ROWS * (j % 4), 1)
                sums = pltpu.roll(sums, PACK - ROWS * (j % 4), 1)
            so[h, j % 4, j // 4] = tokens[:, :HD].T[:ROWS].astype(BF)
            sl[h, j % 4, 4 * (j // 4) : 4 * (j // 4) + 4, :] = sums[:4, :HD]

    def quad_copies(h, other):
        dev = at(quad * 4 + other, y)
        return (
            copy(sl.at[h, other], ql.at[h, seat], qls.at[h, other], qlr.at[h, seat], dev),
            copy(
                so.at[h, other], qo.at[h, seat, :, pl.ds(0, ROWS), :], qos.at[h, other],
                qor.at[h, seat], dev,
            ),
        )

    def quad_wait(h, other):
        part = ql.at[h, other]
        copy(part, part, qls.at[h, other], qlr.at[h, other], across).wait_recv()
        part = qo.at[h, other, :, pl.ds(0, ROWS), :]
        copy(part, part, qos.at[h, other], qor.at[h, other], across).wait_recv()

    def to_quad(h):
        for i in (3, 2, 1):
            for each in quad_copies(h, (seat + i) % 4):
                each.start()
        ql[h, seat] = sl[h, seat]
        qo[h, seat, :, 0:ROWS, :] = so[h, seat]

    def spread(weight, first_row, rows):
        at_row = lax.broadcasted_iota(jnp.int32, (rows, HD), 0) + first_row
        at_col = lax.broadcasted_iota(jnp.int32, (rows, HD), 1)
        return jnp.where(at_row == at_col, weight, 0.0).astype(BF)

    def final_copies(h, k, there):
        dev = (at(over, y), across, across_over)[there]
        rows = theirs if there else mine
        return (
            copy(ml.at[h, k], fl.at[zh, h, quad], fls.at[h, there], flr.at[zh, h, quad], dev),
            copy(
                mo.at[h, k, rows, :], fo.at[zh, h, quad, rows, :], fos.at[h, there],
                for_.at[zh, h, quad], dev,
            ),
        )

    ways = ((2, 1), (1, 0), (0, 1))

    def reduce(h):
        for i in (1, 2, 3):
            quad_wait(h, (seat + i) % 4)
        for k in (1, 0):
            slot = (quad + k) % 2
            row = pl.ds(slot * 4, 1)
            parts = [ql[h, i, row, :] for i in range(4)]
            whole = lse2(*parts)
            weights = jnp.concatenate(
                [spread(jnp.exp2(p - whole), 0, ROWS) for p in parts], axis=1
            )
            mo[h, k] = jnp.dot(
                weights, qo[h, :, slot].reshape(4 * HD, HD), preferred_element_type=F32
            ).astype(BF)
            ml[h, k] = jnp.broadcast_to(whole, (8, HD))
            for there, which in ways:
                if which == k:
                    for each in final_copies(h, k, there):
                        each.start()
        fl[zh, h, quad] = ml[h, 0]
        fo[zh, h, quad, mine, :] = mo[h, 0, mine, :]

    def final_wait(half, h, which):
        part = fl.at[half, h, which]
        copy(part, part, fls.at[h, 0], flr.at[half, h, which], across).wait_recv()
        part = fo.at[half, h, which, mine, :]
        copy(part, part, fos.at[h, 0], for_.at[half, h, which], across).wait_recv()

    def finish(h):
        final_wait(zh, h, 1 - quad)
        final_wait(1 - zh, h, 0)
        final_wait(1 - zh, h, 1)
        for half in range(2):
            parts = [fl[half, h, i, 0:1, :] for i in range(2)]
            whole = lse2(*parts)
            weights = jnp.concatenate(
                [spread(jnp.exp2(p - whole), zh * HALF, HALF) for p in parts], axis=1
            )
            dense[half, 0, :, h * HD : (h + 1) * HD] = jnp.dot(
                weights, fo[half, h].reshape(2 * HD, HD), preferred_element_type=F32
            )

    def gather_tick(e, carry):
        gather_step(e)

        @pl.when(e == 1)
        def _():
            relay(0)

        @pl.when(e == 2)
        def _():
            step2_wait(1, 2)
            akv[y] = local[1:3]
            for i in (1, 3):
                a_copy(i).start()

        @pl.when(e == 3)
        def _():
            for part, i in ((0, 1), (1, 3)):
                a_wait(i)
                a_relay((y + NY - i) % NY, part).start()

        @pl.when(e == 4)
        def _():
            relay(1)

        @pl.when(e == 5)
        def _():
            for i in (1, 3):
                k_copy(2, i).start()
                v_copy(2, i).start()

        return carry

    lax.fori_loop(1, NZ, gather_tick, 0)

    for half in range(2):
        @pl.when(z // 2 + 4 * half != z)
        def _():
            evict_z(half).start()

    @pl.when(jnp.logical_or(z == 0, z == NZ - 1))
    def _():
        evict_own().start()

    for part in range(2):
        a_relay((y + 2) % NY, part).wait_recv()
    for h in range(HEADS):
        values = akv[:, 1, :, h * HD : (h + 1) * HD].reshape(PACK, HD)
        vta[h, 0:HD, :] = values.astype(F32).T.astype(BF)

    def whole_head(h, carry):
        for part in range(2):
            relay_wait(h, part)
        attend(h, (0, 1, 3, 2), True, True)
        to_quad(h)
        return carry

    lax.fori_loop(0, 2, whole_head, 0)
    relay(2)
    attend(2, (0, 1, 3), True, False)
    reduce(0)
    reduce(1)
    for part in range(2):
        relay_wait(2, part)
    attend(2, (2,), False, True)
    to_quad(2)

    for which in range(2):
        @pl.when(2 * (z % 4) + which != z)
        def _():
            rows = evict_rows(which, y)
            copy(rows, rows, ezs.at[0], ezr.at[which], across).wait_recv()

    @pl.when(jnp.logical_or(z == 0, z == NZ - 1))
    def _():
        evict_own().wait()

    for which in range(2):
        for i in (1, 3):
            evict_y(which, i).start()

    finish(0)
    finish(1)
    reduce(2)
    for which, i in ((0, 1), (1, 3)):
        evict_y_wait(which, i)
        evict_relay(which, (y + NY - i) % NY).start()
    finish(2)

    def return1(other):
        return copy(
            packb.at[other, pl.ds(0, BACK1), :], recv2.at[xc], ds.at[other], dr.at[xc],
            beside(other),
        )

    def return1_wait(other):
        part = recv2.at[other]
        copy(part, part, ds.at[other], dr.at[other], beside(other)).wait_recv()

    for i in range(1, NXC):
        step1((xc + i) % NXC).wait_send()
    for d in range(NXC):
        for half in range(2):
            for h in range(HEADS):
                row = (half * HEADS + h) * TOK
                pack32[d, row : row + TOK, :] = dense[
                    half, 0, d * TOK : (d + 1) * TOK, h * HD : (h + 1) * HD
                ]
        packb[d, 0:BACK1, :] = pack32[d, 0:BACK1, :].astype(BF)
    for i in range(1, NXC):
        return1((xc + i) % NXC).start()
    recv2[xc] = packb[xc, 0:BACK1, :]
    for i in range(1, NXC):
        return1_wait((xc + i) % NXC)
    for s in range(NXC):
        pack32[s, 0:BACK1, :] = recv2[s].astype(F32)
        for half in range(2):
            for h in range(HEADS):
                row = (half * HEADS + h) * TOK
                col = ((half * NXC + s) * HEADS + h) * HD
                out_ref[:, col : col + HD] = pack32[s, row : row + TOK, :]

    evict_y_wait(1, 1)
    evict_y_wait(0, 3)
    for which in range(2):
        evict_relay(which, (y + 2) % NY).wait_recv()
    for h in range(HEADS):
        for i in (1, 2, 3):
            for each in quad_copies(h, (seat + i) % 4):
                each.wait_send()
        for there, k in ways:
            for each in final_copies(h, k, there):
                each.wait_send()
    step2(0, 1).wait_send()
    step2(1, 2).wait_send()
    for i in range(1, NXC):
        return1((xc + i) % NXC).wait_send()
    for i in (1, 3):
        a_copy(i).wait_send()
        for which in range(2):
            evict_y(which, i).wait_send()
        for h in range(HEADS):
            k_copy(h, i).wait_send()
            v_copy(h, i).wait_send()
    for part, i in ((0, 1), (1, 3)):
        src = (y + NY - i) % NY
        a_relay(src, part).wait_send()
        evict_relay(part, src).wait_send()
        for h in range(HEADS):
            for each in relay_copies(src, h, part):
                each.wait_send()
    for half in range(2):
        @pl.when(z // 2 + 4 * half != z)
        def _():
            evict_z(half).wait_send()

    def drain(block, carry):
        for h in range(HEADS):
            @pl.when(jnp.logical_and(block <= z, z < NZ - 1))
            def _():
                z_copy(block, h, 0).wait_send()

            @pl.when(jnp.logical_and(block >= z, z > 0))
            def _():
                z_copy(block, h, 1).wait_send()

        return carry

    lax.fori_loop(0, NZ, drain, 0)


def attention(x, window, owner, oldest, slopes):
    dma = pltpu.SemaphoreType.DMA
    vm = pltpu.VMEM
    in_vmem = pl.BlockSpec(memory_space=pltpu.VMEM)
    in_any = pl.BlockSpec(memory_space=pl.ANY)
    return pl.pallas_call(
        kernel,
        out_shape=(
            jax.ShapeDtypeStruct((TOK, 2 * NXC * SHARE), F32),
            jax.ShapeDtypeStruct((2, CACHE, SHARE), BF),
            jax.ShapeDtypeStruct((8, HD), F32),
        ),
        in_specs=[in_any] * 5,
        out_specs=(in_vmem, in_any, in_vmem),
        scratch_shapes=[
            vm((3, TOK, 2 * NXC * SHARE), BF),
            vm((CACHE, SHARE), BF),
            pltpu.SMEM((NZ * NY,), jnp.int32),
            pltpu.SMEM((1,), jnp.int32),
            pltpu.SMEM((2 * NXC * HEADS,), F32),
            dma((8,)),
            vm((NXC, OUT1, HD), F32),
            vm((NXC, OUT1, HD), BF),
            vm((NXC, OUT1, HD), BF),
            vm((2, 3, HALF, SHARE), F32),
            vm((3, ROWS, SHARE), BF),
            vm((NZ, ROWS, SHARE), BF),
            vm((NY, HEADS, CACHE, HD), BF),
            vm((NY, HEADS, SUMS, CACHE), BF),
            vm((NY, 2, ROWS, SHARE), BF),
            vm((HEADS, SUMS, PACK), BF),
            vm((SUMS, NZ * ROWS), F32),
            vm((8, NZ * ROWS), F32),
            vm((HEADS, 4, 2, ROWS, HD), BF),
            vm((HEADS, 4, 8, HD), F32),
            vm((HEADS, 4, 2, HD, HD), BF),
            vm((HEADS, 4, 8, HD), F32),
            vm((HEADS, 2, ROWS, HD), BF),
            vm((HEADS, 2, 8, HD), F32),
            vm((2, HEADS, 2, HD, HD), BF),
            vm((2, HEADS, 2, 8, HD), F32),
            vm((3, HALF, SHARE), BF),
            vm((NXC, BACK1, HD), BF),
            dma((NXC,)), dma((NXC,)),
            dma((3,)), dma((3,)),
            dma((2, NZ, HEADS)), dma((NZ, HEADS)),
            dma((NY, HEADS)), dma((NY, HEADS)), dma((NY, HEADS)), dma((NY, HEADS)),
            dma((2, HEADS)), dma((2, HEADS)), dma((2, HEADS)), dma((2, HEADS)),
            dma((NY,)), dma((NY,)), dma((2,)), dma((2,)),
            dma((HEADS, 4)), dma((HEADS, 4)), dma((HEADS, 4)), dma((HEADS, 4)),
            dma((HEADS, 3)), dma((2, HEADS, 2)), dma((HEADS, 3)), dma((2, HEADS, 2)),
            dma((2,)), dma((2,)), dma((2, NY)), dma((2, NY)),
            dma((2,)), dma((2,)),
            dma((NXC,)), dma((NXC,)), dma(()),
        ],
        compiler_params=pltpu.CompilerParams(
            collective_id=0, has_side_effects=True, vmem_limit_bytes=60 * 1024 * 1024
        ),
        cost_estimate=pl.CostEstimate(
            flops=4 * 3072 * 864 * SHARE, bytes_accessed=4 * 2**20, transcendentals=3072 * 864 * 3
        ),
    )(x, window, owner, oldest, slopes)


def body(active_qkv, window_kv, slot_owner, oldest_slot, timestep, time_slopes, gate_table):
    combined, moved, flag = attention(active_qkv, window_kv, slot_owner, oldest_slot, time_slopes)
    new_window = jnp.where(flag[0, 0] > 0, moved, window_kv)
    gate = lax.dynamic_slice_in_dim(gate_table, timestep[0], 1, 0)
    return ((gate * combined).astype(BF), new_window)


def solution(mesh):
    in_specs = (P(None, ("grp", "sp"), None), P(None, "grp", "sp"), P(), P(), P(), P(), P())
    out_specs = (P(("grp", "sp"), None), P(None, "grp", "sp"))
    return jax.shard_map(body, mesh=mesh, in_specs=in_specs, out_specs=out_specs, check_vma=False)
```

```python
import functools
import math

import jax
import jax.numpy as jnp
from jax import lax
from jax.experimental import pallas as pl
from jax.experimental.pallas import tpu as pltpu
from jax.sharding import PartitionSpec as P

HD = 128
WIN = 8
HEADS = 3
SHARE = HEADS * HD
TOK = 6
ROWS = 96
HALF = 48
CACHE = 768
NZ = 8
NY = 4
NXC = 8
PACK = 4 * ROWS
OUT1 = 112
BACK1 = 48
SUMS = HD + 16
LOG2E = math.log2(math.e)
COEF = LOG2E / math.sqrt(HD)
NONE = -1e30
MESH = pl.DeviceIdType.MESH
BF = jnp.bfloat16
F32 = jnp.float32
NT = (((1,), (1,)), ((), ()))


def lse2(*parts):
    top = functools.reduce(jnp.maximum, parts)
    return top + jnp.log2(sum(jnp.exp2(p - top) for p in parts))


def kernel(
    x_hbm, win_ref, owner_hbm, oldest_hbm, slope_hbm, out_ref, moved_ref, flag_ref,
    x_ref, vbuf, owner_ref, oldest_ref, slope_ref, in_sem,
    pack32, packb, recv1, dense, qbuf, kbuf, vt, akv, vta, acc_ref, top_ref,
    so, sl, qo, ql, mo, ml, fo, fl, back, recv2,
    s1s, s1r, s2s, s2r, sas, sar, sbs, sbr, ks, kr, vs, vr, k2s, k2r, v2s, v2r, acs, acr, a2s, a2r,
    qos, qor, qls, qlr, fos, for_, fls, flr, ezs, ezr, eys, eyr, e2s, e2r, ds, dr, cp_sem,
):
    me = lax.axis_index("grp")
    sp = lax.axis_index("sp")
    z = me // NY
    y = me % NY
    zh = sp // NXC
    xc = sp % NXC
    quad = z // 4
    seat = z % 4

    def at(zz, yy):
        return {"grp": zz * NY + yy, "sp": sp}

    def beside(other):
        return {"grp": me, "sp": zh * NXC + other}

    across = {"grp": me, "sp": (1 - zh) * NXC + xc}
    over = (z + 4) % NZ
    across_over = {"grp": over * NY + y, "sp": (1 - zh) * NXC + xc}

    def copy(src, dst, send, recv, dev):
        return pltpu.make_async_remote_copy(
            src_ref=src, dst_ref=dst, send_sem=send, recv_sem=recv,
            device_id=dev, device_id_type=MESH,
        )

    def head_cols(h):
        return pl.ds(pl.multiple_of(h * HD, HD), HD)

    loads = [
        pltpu.make_async_copy(src, dst, in_sem.at[i])
        for i, (src, dst) in enumerate(
            [
                (x_hbm, x_ref), (win_ref.at[1], vbuf), (owner_hbm, owner_ref),
                (oldest_hbm, oldest_ref), (slope_hbm, slope_ref),
            ]
            + [(win_ref.at[0, :, h * HD : (h + 1) * HD], kbuf.at[y, h]) for h in range(HEADS)]
        )
    ]
    for load in loads:
        load.start()

    barrier = pltpu.get_barrier_semaphore()
    peers = [at((z + i) % NZ, y) for i in range(1, NZ)]
    peers += [at(z, (y + i) % NY) for i in range(1, NY)]
    peers += [beside((xc + i) % NXC) for i in range(1, NXC)]
    peers += [across, across_over]
    for peer in peers:
        pl.semaphore_signal(barrier, inc=1, device_id=peer, device_id_type=MESH)
    pl.semaphore_wait(barrier, len(peers))

    def k_copy(h, i):
        return copy(
            win_ref.at[0, :, h * HD : (h + 1) * HD], kbuf.at[y, h], ks.at[i, h], kr.at[i, h],
            at(z, (y + i) % NY),
        )

    def v_copy(h, i):
        return copy(
            vt.at[y, h, pl.ds(0, HD), :], vt.at[y, h, pl.ds(0, HD), :], vs.at[i, h], vr.at[i, h],
            at(z, (y + i) % NY),
        )

    def kv_wait(h, i):
        src = (y + NY - i) % NY
        copy(kbuf.at[src, h], kbuf.at[src, h], ks.at[i, h], kr.at[i, h], at(z, src)).wait_recv()
        rows = vt.at[src, h, pl.ds(0, HD), :]
        copy(rows, rows, vs.at[i, h], vr.at[i, h], at(z, src)).wait_recv()

    def halves(src, h, part):
        rows = pl.ds(part * PACK, PACK)
        return kbuf.at[src, h, rows, :], vt.at[src, h, pl.ds(0, HD), rows]

    def relay_copies(src, h, part):
        dev = at(z, (y + 1 + 2 * part) % NY)
        keys, values = halves(src, h, part)
        return (
            copy(keys, keys, k2s.at[part, h], k2r.at[part, h], dev),
            copy(values, values, v2s.at[part, h], v2r.at[part, h], dev),
        )

    def relay(h):
        for part, i in ((0, 1), (1, 3)):
            kv_wait(h, i)
            for each in relay_copies((y + NY - i) % NY, h, part):
                each.start()

    def relay_wait(h, part):
        for each in relay_copies((y + 2) % NY, h, part):
            each.wait_recv()

    for i in (1, 3):
        k_copy(0, i).start()

    def step1(other):
        return copy(packb.at[other], recv1.at[xc], s1s.at[other], s1r.at[xc], beside(other))

    def step1_wait(other):
        copy(recv1.at[other], recv1.at[other], s1s.at[other], s1r.at[other], beside(other)).wait_recv()

    def piece(half, t, h):
        return half * 54 + (t * HEADS + h) * TOK

    loads[0].wait()
    for d in range(NXC):
        for half in range(2):
            for t in range(3):
                for h in range(HEADS):
                    col = ((half * NXC + d) * HEADS + h) * HD
                    row = piece(half, t, h)
                    pack32[d, row : row + TOK, :] = x_ref[t, :, col : col + HD].astype(F32)
        packb[d] = pack32[d].astype(BF)
    for i in range(1, NXC):
        step1((xc + i) % NXC).start()
    recv1[xc] = packb[xc]

    loads[1].wait()
    for h in range(HEADS):
        vt[y, h, 0:HD, :] = vbuf[:, h * HD : (h + 1) * HD].astype(F32).T.astype(BF)
        if h < 2:
            for i in (1, 3):
                v_copy(h, i).start()
        if h == 0:
            for i in (1, 3):
                k_copy(1, i).start()
        for src in range(NY):
            vt[src, h, HD:SUMS, :] = jnp.ones((SUMS - HD, CACHE), BF)
        vta[h, HD:SUMS, :] = jnp.ones((SUMS - HD, PACK), BF)
    for load in loads[2:]:
        load.wait()
    flag_ref[...] = jnp.full((1, SHARE), (owner_ref[me] == oldest_ref[0]).astype(F32))

    theirs = pl.ds(pl.multiple_of((1 - zh) * HALF, HALF), HALF)
    for h in range(HEADS):
        for i in range(4):
            qo[h, i, :, ROWS:HD, :] = jnp.zeros((2, HD - ROWS, HD), BF)
        for half in range(2):
            fo[half, h, :, ROWS:HD, :] = jnp.zeros((2, HD - ROWS, HD), BF)
            fo[half, h, :, theirs, :] = jnp.zeros((2, HALF, HD), BF)

    for i in range(1, NXC):
        step1_wait((xc + i) % NXC)
    for s in range(NXC):
        pack32[s] = recv1[s].astype(F32)
    for t in range(3):
        for s in range(NXC):
            for half in range(2):
                for h in range(HEADS):
                    row = piece(half, t, h)
                    dense[half, t, s * TOK : (s + 1) * TOK, h * HD : (h + 1) * HD] = pack32[
                        s, row : row + TOK, :
                    ]

    mine = pl.ds(pl.multiple_of(zh * HALF, HALF), HALF)

    def seat_copy(i):
        src = back.at[0] if i else qbuf.at[z, mine, :]
        dev = (at(over, y), across, across_over)[i]
        return copy(src, qbuf.at[z, mine, :], sas.at[i], sar.at[i], dev)

    def held(i):
        return qbuf.at[
            (over, z, over, z)[i], (mine, theirs, theirs, mine)[i], :
        ]

    def seat_wait(i):
        copy(held(i), held(i), sas.at[i], sar.at[i], across).wait_recv()

    def quad_query(i, other):
        return copy(
            held(i), held(i), sbs.at[i, other], sbr.at[i, seat], at(quad * 4 + other, y)
        )

    def quad_query_wait(i, other):
        block = ((1 - quad, quad, 1 - quad, quad)[i]) * 4 + other
        part = qbuf.at[block, (mine, theirs, theirs, mine)[i], :]
        copy(part, part, sbs.at[i, other], sbr.at[i, other], across).wait_recv()

    def pass_on(i):
        for k in (2, 1, 3):
            quad_query(i, (seat + k) % 4).start()

    back[0] = dense[1 - zh, 0].astype(BF)
    seat_copy(1).start()
    seat_copy(2).start()
    qbuf[z, mine, :] = dense[zh, 0].astype(BF)
    seat_copy(0).start()
    pass_on(3)

    def step2():
        return copy(back.at[pl.ds(1, 2)], akv.at[y, :, mine, :], s2s, s2r, across_over)

    for t in (1, 2):
        back[t] = dense[1 - zh, t].astype(BF)
    step2().start()
    for t in (1, 2):
        akv[y, t - 1, mine, :] = dense[zh, t].astype(BF)

    def a_copy(i):
        return copy(akv.at[y], akv.at[y], acs.at[i], acr.at[i], at(z, (y + i) % NY))

    def a_wait(i):
        src = (y + NY - i) % NY
        copy(akv.at[src], akv.at[src], acs.at[i], acr.at[i], at(z, src)).wait_recv()

    def a_relay(src, part):
        rows = akv.at[src, part]
        return copy(rows, rows, a2s.at[part], a2r.at[part], at(z, (y + 1 + 2 * part) % NY))

    def evict_rows(which, column):
        return moved_ref.at[:, pl.ds((which * NY + column) * ROWS, ROWS), :]

    def evict_part(g):
        base = pl.multiple_of(((z % 2) * NY + y) * ROWS, ROWS)
        place = (zh if g == 0 else 1 - zh) * HALF
        return (
            akv.at[y, :, theirs if g else mine, :],
            moved_ref.at[:, pl.ds(pl.multiple_of(base + place, HALF), HALF), :],
        )

    def evict_target(g, half):
        return (over if g else z) // 2 + 4 * half

    def evict_z(g, half):
        src, dst = evict_part(g)
        return copy(
            src, dst, ezs.at[g, half], ezr.at[z % 2, g], at(evict_target(g, half), y)
        )

    def evict_own(g):
        src, dst = evict_part(g)
        return pltpu.make_async_copy(src, dst, cp_sem)

    def evict_z_wait(which, g):
        group = 2 * seat + which

        @pl.when(group != (over if g else z))
        def _():
            part = akv.at[y, :, mine, :]
            copy(part, part, ezs.at[0, 0], ezr.at[which, g], across).wait_recv()

    def evict_y(which, i):
        rows = evict_rows(which, y)
        return copy(rows, rows, eys.at[which, i], eyr.at[which, i], at(z, (y + i) % NY))

    def evict_relay(which, src):
        rows = evict_rows(which, src)
        return copy(rows, rows, e2s.at[which], e2r.at[which], at(z, (y + 1 + 2 * which) % NY))

    def evict_y_wait(which, i):
        src = (y + NY - i) % NY
        rows = evict_rows(which, src)
        copy(rows, rows, eys.at[which, i], eyr.at[which, i], at(z, src)).wait_recv()

    def attend(h, sources, start, stop):
        cols = head_cols(h)
        q = qbuf[:, :, cols].reshape(NZ * ROWS, HD)
        slope = slope_ref[sp * HEADS + h] * LOG2E

        def window(i, part):
            src = (y + NY - i) % NY
            rows = slice(part * PACK, (part + 1) * PACK)
            slot = owner_ref[z * NY + src] - oldest_ref[0]
            age = WIN - (slot + WIN) % WIN
            return kbuf[src, h, rows, :], vt.at[src, h, :, rows], slope * age.astype(F32)

        chunks = [(akv[:, 0, :, cols].reshape(PACK, HD), vta.at[h], None)] if start else []
        chunks += [window(i, part) for i in sources for part in range(2)]
        top, acc = (None, None) if start else (top_ref[0:1, :], acc_ref[...])
        ahead = lax.dot_general(chunks[0][0], q, NT, preferred_element_type=F32)
        for n, (_, values, bias) in enumerate(chunks):
            score = ahead
            if n + 1 < len(chunks):
                ahead = lax.dot_general(chunks[n + 1][0], q, NT, preferred_element_type=F32)
            new = jnp.max(score, axis=0, keepdims=True) * COEF
            if bias is not None:
                new = new - bias
            if top is not None:
                new = jnp.maximum(top, new)
            weight = jnp.exp2(score * COEF - (new if bias is None else new + bias))
            part = jnp.dot(values[...], weight.astype(BF), preferred_element_type=F32)
            acc = part if top is None else acc * jnp.exp2(top - new) + part
            top = new
        if not stop:
            top_ref[...] = jnp.broadcast_to(top, (8, NZ * ROWS))
            acc_ref[...] = acc
            return
        total = acc[HD : HD + 1]
        mixed = acc[:HD] * (1.0 / total)
        lse = jnp.broadcast_to(top + jnp.log2(total), (8, NZ * ROWS))
        for j in range(NZ):
            pack = slice(j // 4 * PACK, (j // 4 + 1) * PACK)
            tokens, sums = mixed[:, pack], lse[:, pack]
            if j % 4:
                tokens = pltpu.roll(tokens, PACK - ROWS * (j % 4), 1)
                sums = pltpu.roll(sums, PACK - ROWS * (j % 4), 1)
            so[h, j % 4, j // 4] = tokens[:, :HD].T[:ROWS].astype(BF)
            sl[h, j % 4, 4 * (j // 4) : 4 * (j // 4) + 4, :] = sums[:4, :HD]

    def quad_copies(h, other):
        dev = at(quad * 4 + other, y)
        return (
            copy(sl.at[h, other], ql.at[h, seat], qls.at[h, other], qlr.at[h, seat], dev),
            copy(
                so.at[h, other], qo.at[h, seat, :, pl.ds(0, ROWS), :], qos.at[h, other],
                qor.at[h, seat], dev,
            ),
        )

    def quad_wait(h, other):
        part = ql.at[h, other]
        copy(part, part, qls.at[h, other], qlr.at[h, other], across).wait_recv()
        part = qo.at[h, other, :, pl.ds(0, ROWS), :]
        copy(part, part, qos.at[h, other], qor.at[h, other], across).wait_recv()

    def to_quad(h):
        for i in (3, 2, 1):
            for each in quad_copies(h, (seat + i) % 4):
                each.start()
        ql[h, seat] = sl[h, seat]
        qo[h, seat, :, 0:ROWS, :] = so[h, seat]

    def spread(weight, first_row, rows):
        at_row = lax.broadcasted_iota(jnp.int32, (rows, HD), 0) + first_row
        at_col = lax.broadcasted_iota(jnp.int32, (rows, HD), 1)
        return jnp.where(at_row == at_col, weight, 0.0).astype(BF)

    def final_copies(h, k, there):
        dev = (at(over, y), across, across_over)[there]
        rows = theirs if there else mine
        return (
            copy(ml.at[h, k], fl.at[zh, h, quad], fls.at[h, there], flr.at[zh, h, quad], dev),
            copy(
                mo.at[h, k, rows, :], fo.at[zh, h, quad, rows, :], fos.at[h, there],
                for_.at[zh, h, quad], dev,
            ),
        )

    ways = ((2, 1), (1, 0), (0, 1))

    def reduce(h):
        for i in (1, 2, 3):
            quad_wait(h, (seat + i) % 4)
        for k in (1, 0):
            slot = (quad + k) % 2
            row = pl.ds(slot * 4, 1)
            parts = [ql[h, i, row, :] for i in range(4)]
            whole = lse2(*parts)
            weights = jnp.concatenate(
                [spread(jnp.exp2(p - whole), 0, ROWS) for p in parts], axis=1
            )
            mo[h, k] = jnp.dot(
                weights, qo[h, :, slot].reshape(4 * HD, HD), preferred_element_type=F32
            ).astype(BF)
            ml[h, k] = jnp.broadcast_to(whole, (8, HD))
            for there, which in ways:
                if which == k:
                    for each in final_copies(h, k, there):
                        each.start()
        fl[zh, h, quad] = ml[h, 0]
        fo[zh, h, quad, mine, :] = mo[h, 0, mine, :]

    def final_wait(half, h, which):
        part = fl.at[half, h, which]
        copy(part, part, fls.at[h, 0], flr.at[half, h, which], across).wait_recv()
        part = fo.at[half, h, which, mine, :]
        copy(part, part, fos.at[h, 0], for_.at[half, h, which], across).wait_recv()

    def finish(h):
        final_wait(zh, h, 1 - quad)
        final_wait(1 - zh, h, 0)
        final_wait(1 - zh, h, 1)
        for half in range(2):
            parts = [fl[half, h, i, 0:1, :] for i in range(2)]
            whole = lse2(*parts)
            weights = jnp.concatenate(
                [spread(jnp.exp2(p - whole), zh * HALF, HALF) for p in parts], axis=1
            )
            dense[half, 0, :, h * HD : (h + 1) * HD] = jnp.dot(
                weights, fo[half, h].reshape(2 * HD, HD), preferred_element_type=F32
            )

    seat_wait(0)
    pass_on(0)
    seat_wait(2)
    pass_on(2)
    relay(0)
    seat_wait(1)
    pass_on(1)
    part = akv.at[y, :, theirs, :]
    copy(part, part, s2s, s2r, across).wait_recv()
    for i in (1, 3):
        a_copy(i).start()
    for part, i in ((0, 1), (1, 3)):
        a_wait(i)
        a_relay((y + NY - i) % NY, part).start()
    relay(1)
    for i in (1, 3):
        k_copy(2, i).start()
        v_copy(2, i).start()
    for i in (3, 0, 2, 1):
        for k in (1, 2, 3):
            quad_query_wait(i, (seat + k) % 4)

    for g in range(2):
        for half in range(2):
            @pl.when(evict_target(g, half) != z)
            def _():
                evict_z(g, half).start()

            @pl.when(evict_target(g, half) == z)
            def _():
                evict_own(g).start()

    for part in range(2):
        a_relay((y + 2) % NY, part).wait_recv()
    for h in range(HEADS):
        values = akv[:, 1, :, h * HD : (h + 1) * HD].reshape(PACK, HD)
        vta[h, 0:HD, :] = values.astype(F32).T.astype(BF)

    def whole_head(h, carry):
        for part in range(2):
            relay_wait(h, part)
        attend(h, (0, 1, 3, 2), True, True)
        to_quad(h)
        return carry

    lax.fori_loop(0, 2, whole_head, 0)
    relay(2)
    attend(2, (0, 1, 3), True, False)
    reduce(0)
    reduce(1)
    for part in range(2):
        relay_wait(2, part)
    attend(2, (2,), False, True)
    to_quad(2)

    reduce(2)
    for which in range(2):
        for g in range(2):
            evict_z_wait(which, g)

    for g in range(2):
        for half in range(2):
            @pl.when(evict_target(g, half) == z)
            def _():
                evict_own(g).wait()

    for which in range(2):
        for i in (1, 3):
            evict_y(which, i).start()

    finish(0)
    finish(1)
    for which, i in ((0, 1), (1, 3)):
        evict_y_wait(which, i)
        evict_relay(which, (y + NY - i) % NY).start()
    finish(2)

    def return1(other):
        return copy(
            packb.at[other, pl.ds(0, BACK1), :], recv2.at[xc], ds.at[other], dr.at[xc],
            beside(other),
        )

    def return1_wait(other):
        part = recv2.at[other]
        copy(part, part, ds.at[other], dr.at[other], beside(other)).wait_recv()

    for i in range(1, NXC):
        step1((xc + i) % NXC).wait_send()
    for d in range(NXC):
        for half in range(2):
            for h in range(HEADS):
                row = (half * HEADS + h) * TOK
                pack32[d, row : row + TOK, :] = dense[
                    half, 0, d * TOK : (d + 1) * TOK, h * HD : (h + 1) * HD
                ]
        packb[d, 0:BACK1, :] = pack32[d, 0:BACK1, :].astype(BF)
    for i in range(1, NXC):
        return1((xc + i) % NXC).start()
    recv2[xc] = packb[xc, 0:BACK1, :]
    for i in range(1, NXC):
        return1_wait((xc + i) % NXC)
    for s in range(NXC):
        pack32[s, 0:BACK1, :] = recv2[s].astype(F32)
        for half in range(2):
            for h in range(HEADS):
                row = (half * HEADS + h) * TOK
                col = ((half * NXC + s) * HEADS + h) * HD
                out_ref[:, col : col + HD] = pack32[s, row : row + TOK, :]

    evict_y_wait(1, 1)
    evict_y_wait(0, 3)
    for which in range(2):
        evict_relay(which, (y + 2) % NY).wait_recv()
    for h in range(HEADS):
        for i in (1, 2, 3):
            for each in quad_copies(h, (seat + i) % 4):
                each.wait_send()
        for there, k in ways:
            for each in final_copies(h, k, there):
                each.wait_send()
    step2().wait_send()
    for i in range(3):
        seat_copy(i).wait_send()
    for i in range(4):
        for k in (1, 2, 3):
            quad_query(i, (seat + k) % 4).wait_send()
    for i in range(1, NXC):
        return1((xc + i) % NXC).wait_send()
    for i in (1, 3):
        a_copy(i).wait_send()
        for which in range(2):
            evict_y(which, i).wait_send()
        for h in range(HEADS):
            k_copy(h, i).wait_send()
            v_copy(h, i).wait_send()
    for part, i in ((0, 1), (1, 3)):
        src = (y + NY - i) % NY
        a_relay(src, part).wait_send()
        evict_relay(part, src).wait_send()
        for h in range(HEADS):
            for each in relay_copies(src, h, part):
                each.wait_send()
    for g in range(2):
        for half in range(2):
            @pl.when(evict_target(g, half) != z)
            def _():
                evict_z(g, half).wait_send()


def attention(x, window, owner, oldest, slopes):
    dma = pltpu.SemaphoreType.DMA
    vm = pltpu.VMEM
    in_vmem = pl.BlockSpec(memory_space=pltpu.VMEM)
    in_any = pl.BlockSpec(memory_space=pl.ANY)
    return pl.pallas_call(
        kernel,
        out_shape=(
            jax.ShapeDtypeStruct((TOK, 2 * NXC * SHARE), F32),
            jax.ShapeDtypeStruct((2, CACHE, SHARE), BF),
            jax.ShapeDtypeStruct((1, SHARE), F32),
        ),
        in_specs=[in_any] * 5,
        out_specs=(in_vmem, in_any, in_vmem),
        scratch_shapes=[
            vm((3, TOK, 2 * NXC * SHARE), BF),
            vm((CACHE, SHARE), BF),
            pltpu.SMEM((NZ * NY,), jnp.int32),
            pltpu.SMEM((1,), jnp.int32),
            pltpu.SMEM((2 * NXC * HEADS,), F32),
            dma((8,)),
            vm((NXC, OUT1, HD), F32),
            vm((NXC, OUT1, HD), BF),
            vm((NXC, OUT1, HD), BF),
            vm((2, 3, HALF, SHARE), F32),
            vm((NZ, ROWS, SHARE), BF),
            vm((NY, HEADS, CACHE, HD), BF),
            vm((NY, HEADS, SUMS, CACHE), BF),
            vm((NY, 2, ROWS, SHARE), BF),
            vm((HEADS, SUMS, PACK), BF),
            vm((SUMS, NZ * ROWS), F32),
            vm((8, NZ * ROWS), F32),
            vm((HEADS, 4, 2, ROWS, HD), BF),
            vm((HEADS, 4, 8, HD), F32),
            vm((HEADS, 4, 2, HD, HD), BF),
            vm((HEADS, 4, 8, HD), F32),
            vm((HEADS, 2, ROWS, HD), BF),
            vm((HEADS, 2, 8, HD), F32),
            vm((2, HEADS, 2, HD, HD), BF),
            vm((2, HEADS, 2, 8, HD), F32),
            vm((3, HALF, SHARE), BF),
            vm((NXC, BACK1, HD), BF),
            dma((NXC,)), dma((NXC,)),
            dma(()), dma(()),
            dma((3,)), dma((3,)), dma((4, 4)), dma((4, 4)),
            dma((NY, HEADS)), dma((NY, HEADS)), dma((NY, HEADS)), dma((NY, HEADS)),
            dma((2, HEADS)), dma((2, HEADS)), dma((2, HEADS)), dma((2, HEADS)),
            dma((NY,)), dma((NY,)), dma((2,)), dma((2,)),
            dma((HEADS, 4)), dma((HEADS, 4)), dma((HEADS, 4)), dma((HEADS, 4)),
            dma((HEADS, 3)), dma((2, HEADS, 2)), dma((HEADS, 3)), dma((2, HEADS, 2)),
            dma((2, 2)), dma((2, 2)), dma((2, NY)), dma((2, NY)),
            dma((2,)), dma((2,)),
            dma((NXC,)), dma((NXC,)), dma(()),
        ],
        compiler_params=pltpu.CompilerParams(
            collective_id=0, has_side_effects=True, vmem_limit_bytes=60 * 1024 * 1024
        ),
        cost_estimate=pl.CostEstimate(
            flops=4 * 3072 * 864 * SHARE, bytes_accessed=4 * 2**20, transcendentals=3072 * 864 * 3
        ),
    )(x, window, owner, oldest, slopes)


def body(active_qkv, window_kv, slot_owner, oldest_slot, timestep, time_slopes, gate_table):
    combined, moved, flag = attention(active_qkv, window_kv, slot_owner, oldest_slot, time_slopes)
    new_window = jnp.where(flag[None] > 0, moved, window_kv)
    gate = lax.dynamic_slice_in_dim(gate_table, timestep[0], 1, 0)
    return ((gate * combined).astype(BF), new_window)


def solution(mesh):
    in_specs = (P(None, ("grp", "sp"), None), P(None, "grp", "sp"), P(), P(), P(), P(), P())
    out_specs = (P(("grp", "sp"), None), P(None, "grp", "sp"))
    return jax.shard_map(body, mesh=mesh, in_specs=in_specs, out_specs=out_specs, check_vma=False)
```

```python
import functools
import math

import jax
import jax.numpy as jnp
from jax import lax
from jax.experimental import pallas as pl
from jax.experimental.pallas import tpu as pltpu
from jax.sharding import PartitionSpec as P

HD = 128
WIN = 8
HEADS = 3
SHARE = HEADS * HD
TOK = 6
ROWS = 96
HALF = 48
CACHE = 768
NZ = 8
NY = 4
NXC = 8
PACK = 4 * ROWS
OUT1 = 112
BACK1 = 48
SUMS = HD + 16
LOG2E = math.log2(math.e)
COEF = LOG2E / math.sqrt(HD)
NONE = -1e30
MESH = pl.DeviceIdType.MESH
BF = jnp.bfloat16
F32 = jnp.float32
NT = (((1,), (1,)), ((), ()))


def lse2(*parts):
    top = functools.reduce(jnp.maximum, parts)
    return top + jnp.log2(sum(jnp.exp2(p - top) for p in parts))


def kernel(
    x_hbm, win_ref, owner_hbm, oldest_hbm, time_hbm, slope_hbm, gate_hbm, out_ref, new_hbm,
    x_ref, vbuf, gate_ref, owner_ref, oldest_ref, time_ref, slope_ref, moved_ref, in_sem, new_sem,
    pack32, packb, recv1, dense, qbuf, kbuf, vt, akv, vta, acc_ref, top_ref,
    so, sl, qo, ql, mo, ml, fo, fl, back, recv2,
    s1s, s1r, s2s, s2r, sas, sar, sbs, sbr, ks, kr, vs, vr, k2s, k2r, v2s, v2r, acs, acr, a2s, a2r,
    qos, qor, qls, qlr, fos, for_, fls, flr, ezs, ezr, eys, eyr, e2s, e2r, ds, dr, cp_sem,
):
    me = lax.axis_index("grp")
    sp = lax.axis_index("sp")
    z = me // NY
    y = me % NY
    zh = sp // NXC
    xc = sp % NXC
    quad = z // 4
    seat = z % 4

    def at(zz, yy):
        return {"grp": zz * NY + yy, "sp": sp}

    def beside(other):
        return {"grp": me, "sp": zh * NXC + other}

    across = {"grp": me, "sp": (1 - zh) * NXC + xc}
    over = (z + 4) % NZ
    across_over = {"grp": over * NY + y, "sp": (1 - zh) * NXC + xc}

    def copy(src, dst, send, recv, dev):
        return pltpu.make_async_remote_copy(
            src_ref=src, dst_ref=dst, send_sem=send, recv_sem=recv,
            device_id=dev, device_id_type=MESH,
        )

    def head_cols(h):
        return pl.ds(pl.multiple_of(h * HD, HD), HD)

    loads = [
        pltpu.make_async_copy(src, dst, in_sem.at[i])
        for i, (src, dst) in enumerate(
            [
                (x_hbm, x_ref), (win_ref.at[1], vbuf), (owner_hbm, owner_ref),
                (oldest_hbm, oldest_ref), (slope_hbm, slope_ref), (time_hbm, time_ref),
                (gate_hbm, gate_ref),
            ]
            + [(win_ref.at[0, :, h * HD : (h + 1) * HD], kbuf.at[y, h]) for h in range(HEADS)]
        )
    ]
    for load in loads:
        load.start()

    barrier = pltpu.get_barrier_semaphore()
    peers = [at((z + i) % NZ, y) for i in range(1, NZ)]
    peers += [at(z, (y + i) % NY) for i in range(1, NY)]
    peers += [beside((xc + i) % NXC) for i in range(1, NXC)]
    peers += [across, across_over]
    for peer in peers:
        pl.semaphore_signal(barrier, inc=1, device_id=peer, device_id_type=MESH)
    pl.semaphore_wait(barrier, len(peers))

    def k_copy(h, i):
        return copy(
            win_ref.at[0, :, h * HD : (h + 1) * HD], kbuf.at[y, h], ks.at[i, h], kr.at[i, h],
            at(z, (y + i) % NY),
        )

    def v_copy(h, i):
        return copy(
            vt.at[y, h, pl.ds(0, HD), :], vt.at[y, h, pl.ds(0, HD), :], vs.at[i, h], vr.at[i, h],
            at(z, (y + i) % NY),
        )

    def kv_wait(h, i):
        src = (y + NY - i) % NY
        copy(kbuf.at[src, h], kbuf.at[src, h], ks.at[i, h], kr.at[i, h], at(z, src)).wait_recv()
        rows = vt.at[src, h, pl.ds(0, HD), :]
        copy(rows, rows, vs.at[i, h], vr.at[i, h], at(z, src)).wait_recv()

    def halves(src, h, part):
        rows = pl.ds(part * PACK, PACK)
        return kbuf.at[src, h, rows, :], vt.at[src, h, pl.ds(0, HD), rows]

    def relay_copies(src, h, part):
        dev = at(z, (y + 1 + 2 * part) % NY)
        keys, values = halves(src, h, part)
        return (
            copy(keys, keys, k2s.at[part, h], k2r.at[part, h], dev),
            copy(values, values, v2s.at[part, h], v2r.at[part, h], dev),
        )

    def relay(h):
        for part, i in ((0, 1), (1, 3)):
            kv_wait(h, i)
            for each in relay_copies((y + NY - i) % NY, h, part):
                each.start()

    def relay_wait(h, part):
        for each in relay_copies((y + 2) % NY, h, part):
            each.wait_recv()

    for i in (1, 3):
        k_copy(0, i).start()

    def step1(other):
        return copy(packb.at[other], recv1.at[xc], s1s.at[other], s1r.at[xc], beside(other))

    def step1_wait(other):
        copy(recv1.at[other], recv1.at[other], s1s.at[other], s1r.at[other], beside(other)).wait_recv()

    def piece(half, t, h):
        return half * 54 + (t * HEADS + h) * TOK

    loads[0].wait()
    for d in range(NXC):
        for half in range(2):
            for t in range(3):
                for h in range(HEADS):
                    col = ((half * NXC + d) * HEADS + h) * HD
                    row = piece(half, t, h)
                    pack32[d, row : row + TOK, :] = x_ref[t, :, col : col + HD].astype(F32)
        packb[d] = pack32[d].astype(BF)
    for i in range(1, NXC):
        step1((xc + i) % NXC).start()
    recv1[xc] = packb[xc]

    loads[1].wait()
    for h in range(HEADS):
        vt[y, h, 0:HD, :] = vbuf[:, h * HD : (h + 1) * HD].astype(F32).T.astype(BF)
        if h < 2:
            for i in (1, 3):
                v_copy(h, i).start()
        if h == 0:
            for i in (1, 3):
                k_copy(1, i).start()
        for src in range(NY):
            vt[src, h, HD:SUMS, :] = jnp.ones((SUMS - HD, CACHE), BF)
        vta[h, HD:SUMS, :] = jnp.ones((SUMS - HD, PACK), BF)
    for load in loads[2:]:
        load.wait()

    theirs = pl.ds(pl.multiple_of((1 - zh) * HALF, HALF), HALF)
    for h in range(HEADS):
        for i in range(4):
            qo[h, i, :, ROWS:HD, :] = jnp.zeros((2, HD - ROWS, HD), BF)
        for half in range(2):
            fo[half, h, :, ROWS:HD, :] = jnp.zeros((2, HD - ROWS, HD), BF)
            fo[half, h, :, theirs, :] = jnp.zeros((2, HALF, HD), BF)

    for i in range(1, NXC):
        step1_wait((xc + i) % NXC)
    for s in range(NXC):
        pack32[s] = recv1[s].astype(F32)
    for t in range(3):
        for s in range(NXC):
            for half in range(2):
                for h in range(HEADS):
                    row = piece(half, t, h)
                    dense[half, t, s * TOK : (s + 1) * TOK, h * HD : (h + 1) * HD] = pack32[
                        s, row : row + TOK, :
                    ]

    mine = pl.ds(pl.multiple_of(zh * HALF, HALF), HALF)

    def seat_copy(i):
        src = back.at[0] if i else qbuf.at[z, mine, :]
        dev = (at(over, y), across, across_over)[i]
        return copy(src, qbuf.at[z, mine, :], sas.at[i], sar.at[i], dev)

    def held(i):
        return qbuf.at[
            (over, z, over, z)[i], (mine, theirs, theirs, mine)[i], :
        ]

    def seat_wait(i):
        copy(held(i), held(i), sas.at[i], sar.at[i], across).wait_recv()

    def quad_query(i, other):
        return copy(
            held(i), held(i), sbs.at[i, other], sbr.at[i, seat], at(quad * 4 + other, y)
        )

    def quad_query_wait(i, other):
        block = ((1 - quad, quad, 1 - quad, quad)[i]) * 4 + other
        part = qbuf.at[block, (mine, theirs, theirs, mine)[i], :]
        copy(part, part, sbs.at[i, other], sbr.at[i, other], across).wait_recv()

    def pass_on(i):
        for k in (2, 1, 3):
            quad_query(i, (seat + k) % 4).start()

    back[0] = dense[1 - zh, 0].astype(BF)
    seat_copy(1).start()
    seat_copy(2).start()
    qbuf[z, mine, :] = dense[zh, 0].astype(BF)
    seat_copy(0).start()

    def step2():
        return copy(back.at[pl.ds(1, 2)], akv.at[y, :, mine, :], s2s, s2r, across_over)

    for t in (1, 2):
        back[t] = dense[1 - zh, t].astype(BF)
    step2().start()
    for t in (1, 2):
        akv[y, t - 1, mine, :] = dense[zh, t].astype(BF)
    pass_on(3)

    def a_copy(i):
        return copy(akv.at[y], akv.at[y], acs.at[i], acr.at[i], at(z, (y + i) % NY))

    def a_wait(i):
        src = (y + NY - i) % NY
        copy(akv.at[src], akv.at[src], acs.at[i], acr.at[i], at(z, src)).wait_recv()

    def a_relay(src, part):
        rows = akv.at[src, part]
        return copy(rows, rows, a2s.at[part], a2r.at[part], at(z, (y + 1 + 2 * part) % NY))

    def evict_rows(which, column):
        return moved_ref.at[:, pl.ds((which * NY + column) * ROWS, ROWS), :]

    def evict_part(g):
        base = pl.multiple_of(((z % 2) * NY + y) * ROWS, ROWS)
        place = (zh if g == 0 else 1 - zh) * HALF
        return (
            akv.at[y, :, theirs if g else mine, :],
            moved_ref.at[:, pl.ds(pl.multiple_of(base + place, HALF), HALF), :],
        )

    def evict_target(g, half):
        return (over if g else z) // 2 + 4 * half

    def evict_z(g, half):
        src, dst = evict_part(g)
        return copy(
            src, dst, ezs.at[g, half], ezr.at[z % 2, g], at(evict_target(g, half), y)
        )

    def evict_own(g):
        src, dst = evict_part(g)
        return pltpu.make_async_copy(src, dst, cp_sem)

    def evict_z_wait(which, g):
        group = 2 * seat + which

        @pl.when(group != (over if g else z))
        def _():
            part = akv.at[y, :, mine, :]
            copy(part, part, ezs.at[0, 0], ezr.at[which, g], across).wait_recv()

    def evict_y(which, i):
        rows = evict_rows(which, y)
        return copy(rows, rows, eys.at[which, i], eyr.at[which, i], at(z, (y + i) % NY))

    def evict_relay(which, src):
        rows = evict_rows(which, src)
        return copy(rows, rows, e2s.at[which], e2r.at[which], at(z, (y + 1 + 2 * which) % NY))

    def evict_y_wait(which, i):
        src = (y + NY - i) % NY
        rows = evict_rows(which, src)
        copy(rows, rows, eys.at[which, i], eyr.at[which, i], at(z, src)).wait_recv()

    def attend(h, active, sources, start, stop):
        cols = head_cols(h)
        q = qbuf[:, :, cols].reshape(NZ * ROWS, HD)
        slope = slope_ref[sp * HEADS + h] * LOG2E

        def window(i, part):
            src = (y + NY - i) % NY
            rows = slice(part * PACK, (part + 1) * PACK)
            slot = owner_ref[z * NY + src] - oldest_ref[0]
            age = WIN - (slot + WIN) % WIN
            return kbuf[src, h, rows, :], vt.at[src, h, :, rows], slope * age.astype(F32)

        chunks = [(akv[:, 0, :, cols].reshape(PACK, HD), vta.at[h], None)] if active else []
        chunks += [window(i, part) for i in sources for part in range(2)]
        top, acc = (None, None) if start else (top_ref[0:1, :], acc_ref[...])
        ahead = lax.dot_general(chunks[0][0], q, NT, preferred_element_type=F32)
        for n, (_, values, bias) in enumerate(chunks):
            score = ahead
            if n + 1 < len(chunks):
                ahead = lax.dot_general(chunks[n + 1][0], q, NT, preferred_element_type=F32)
            new = jnp.max(score, axis=0, keepdims=True) * COEF
            if bias is not None:
                new = new - bias
            if top is not None:
                new = jnp.maximum(top, new)
            weight = jnp.exp2(score * COEF - (new if bias is None else new + bias))
            part = jnp.dot(values[...], weight.astype(BF), preferred_element_type=F32)
            acc = part if top is None else acc * jnp.exp2(top - new) + part
            top = new
        if not stop:
            top_ref[...] = jnp.broadcast_to(top, (8, NZ * ROWS))
            acc_ref[...] = acc
            return
        total = acc[HD : HD + 1]
        mixed = acc[:HD] * (1.0 / total)
        lse = jnp.broadcast_to(top + jnp.log2(total), (8, NZ * ROWS))
        for j in range(NZ):
            pack = slice(j // 4 * PACK, (j // 4 + 1) * PACK)
            tokens, sums = mixed[:, pack], lse[:, pack]
            if j % 4:
                tokens = pltpu.roll(tokens, PACK - ROWS * (j % 4), 1)
                sums = pltpu.roll(sums, PACK - ROWS * (j % 4), 1)
            so[h, j % 4, j // 4] = tokens[:, :HD].T[:ROWS].astype(BF)
            sl[h, j % 4, 4 * (j // 4) : 4 * (j // 4) + 4, :] = sums[:4, :HD]

    def quad_lse(h, other):
        return copy(
            sl.at[h, other], ql.at[h, seat], qls.at[h, other], qlr.at[h, seat],
            at(quad * 4 + other, y),
        )

    def quad_part(h, slot, other):
        return copy(
            so.at[h, other, slot], qo.at[h, seat, slot, pl.ds(0, ROWS), :],
            qos.at[h, slot, other], qor.at[h, slot, seat], at(quad * 4 + other, y),
        )

    def quad_wait(h, slot, other):
        part = qo.at[h, other, slot, pl.ds(0, ROWS), :]
        copy(part, part, qos.at[h, slot, other], qor.at[h, slot, other], across).wait_recv()

    def quad_lse_wait(h, other):
        part = ql.at[h, other]
        copy(part, part, qls.at[h, other], qlr.at[h, other], across).wait_recv()

    def to_quad(h):
        for i in (2, 1, 3):
            quad_lse(h, (seat + i) % 4).start()
        for slot in (quad, 1 - quad):
            for i in (2, 1, 3):
                quad_part(h, slot, (seat + i) % 4).start()
        ql[h, seat] = sl[h, seat]
        qo[h, seat, :, 0:ROWS, :] = so[h, seat]

    def spread(weight, first_row, rows):
        at_row = lax.broadcasted_iota(jnp.int32, (rows, HD), 0) + first_row
        at_col = lax.broadcasted_iota(jnp.int32, (rows, HD), 1)
        return jnp.where(at_row == at_col, weight, 0.0).astype(BF)

    def final_copies(h, k, there):
        dev = (at(over, y), across, across_over)[there]
        rows = theirs if there else mine
        return (
            copy(ml.at[h, k], fl.at[zh, h, quad], fls.at[h, there], flr.at[zh, h, quad], dev),
            copy(
                mo.at[h, k, rows, :], fo.at[zh, h, quad, rows, :], fos.at[h, there],
                for_.at[zh, h, quad], dev,
            ),
        )

    ways = ((2, 1), (1, 0), (0, 1))

    def reduce(h):
        for i in (1, 3, 2):
            quad_lse_wait(h, (seat + i) % 4)
        for k in (0, 1):
            slot = (quad + k) % 2
            for i in (1, 3, 2):
                quad_wait(h, slot, (seat + i) % 4)
            row = pl.ds(slot * 4, 1)
            parts = [ql[h, i, row, :] for i in range(4)]
            whole = lse2(*parts)
            weights = jnp.concatenate(
                [spread(jnp.exp2(p - whole), 0, ROWS) for p in parts], axis=1
            )
            mo[h, k] = jnp.dot(
                weights, qo[h, :, slot].reshape(4 * HD, HD), preferred_element_type=F32
            ).astype(BF)
            ml[h, k] = jnp.broadcast_to(whole, (8, HD))
            for there, which in ways:
                if which == k:
                    for each in final_copies(h, k, there):
                        each.start()
        fl[zh, h, quad] = ml[h, 0]
        fo[zh, h, quad, mine, :] = mo[h, 0, mine, :]

    def final_wait(half, h, which):
        part = fl.at[half, h, which]
        copy(part, part, fls.at[h, 0], flr.at[half, h, which], across).wait_recv()
        part = fo.at[half, h, which, mine, :]
        copy(part, part, fos.at[h, 0], for_.at[half, h, which], across).wait_recv()

    def finish(h):
        final_wait(zh, h, 1 - quad)
        final_wait(1 - zh, h, 0)
        final_wait(1 - zh, h, 1)
        for half in range(2):
            parts = [fl[half, h, i, 0:1, :] for i in range(2)]
            whole = lse2(*parts)
            weights = jnp.concatenate(
                [spread(jnp.exp2(p - whole), zh * HALF, HALF) for p in parts], axis=1
            )
            dense[half, 0, :, h * HD : (h + 1) * HD] = jnp.dot(
                weights, fo[half, h].reshape(2 * HD, HD), preferred_element_type=F32
            )

    seat_wait(0)
    pass_on(0)
    seat_wait(2)
    pass_on(2)
    relay(0)
    seat_wait(1)
    pass_on(1)
    for i in (1, 3):
        k_copy(2, i).start()
    part = akv.at[y, :, theirs, :]
    copy(part, part, s2s, s2r, across).wait_recv()
    for i in (1, 3):
        a_copy(i).start()
    for g in range(2):
        for half in range(2):
            @pl.when(evict_target(g, half) != z)
            def _():
                evict_z(g, half).start()

            @pl.when(evict_target(g, half) == z)
            def _():
                evict_own(g).start()

    relay(1)
    for part, i in ((0, 1), (1, 3)):
        a_wait(i)
        a_relay((y + NY - i) % NY, part).start()
    for i in (1, 3):
        v_copy(2, i).start()
    for i in (3, 0, 2, 1):
        for k in (1, 2, 3):
            quad_query_wait(i, (seat + k) % 4)

    for part in range(2):
        a_relay((y + 2) % NY, part).wait_recv()
    for h in range(HEADS):
        values = akv[:, 1, :, h * HD : (h + 1) * HD].reshape(PACK, HD)
        vta[h, 0:HD, :] = values.astype(F32).T.astype(BF)
    for h in range(2):
        for part in range(2):
            relay_wait(h, part)
        attend(h, True, (0, 1, 3, 2), True, True)
        to_quad(h)
    relay(2)
    attend(2, True, (0, 1, 3), True, False)
    reduce(0)
    for part in range(2):
        relay_wait(2, part)
    attend(2, False, (2,), False, True)
    to_quad(2)
    reduce(1)

    for which in range(2):
        for g in range(2):
            evict_z_wait(which, g)

    for g in range(2):
        for half in range(2):
            @pl.when(evict_target(g, half) == z)
            def _():
                evict_own(g).wait()

    for which in range(2):
        for i in (1, 3):
            evict_y(which, i).start()

    reduce(2)
    finish(0)
    finish(1)
    for which, i in ((0, 1), (1, 3)):
        evict_y_wait(which, i)
        evict_relay(which, (y + NY - i) % NY).start()
    finish(2)

    def return1(other):
        return copy(
            packb.at[other, pl.ds(0, BACK1), :], recv2.at[xc], ds.at[other], dr.at[xc],
            beside(other),
        )

    def return1_wait(other):
        part = recv2.at[other]
        copy(part, part, ds.at[other], dr.at[other], beside(other)).wait_recv()

    for i in range(1, NXC):
        step1((xc + i) % NXC).wait_send()
    for d in range(NXC):
        for half in range(2):
            for h in range(HEADS):
                row = (half * HEADS + h) * TOK
                pack32[d, row : row + TOK, :] = dense[
                    half, 0, d * TOK : (d + 1) * TOK, h * HD : (h + 1) * HD
                ]
        packb[d, 0:BACK1, :] = pack32[d, 0:BACK1, :].astype(BF)
    for i in range(1, NXC):
        return1((xc + i) % NXC).start()
    recv2[xc] = packb[xc, 0:BACK1, :]
    evict_y_wait(1, 1)
    evict_y_wait(0, 3)
    for which in range(2):
        evict_relay(which, (y + 2) % NY).wait_recv()
    for which, i in ((0, 1), (1, 3)):
        evict_relay(which, (y + NY - i) % NY).wait_send()
        for side in (1, 3):
            evict_y(which, side).wait_send()
    evicted = owner_ref[me] == oldest_ref[0]
    for h in range(HEADS):
        cols = slice(h * HD, (h + 1) * HD)
        moved_ref[0, :, cols] = jnp.where(evicted, moved_ref[0, :, cols], kbuf[y, h])
    moved_ref[1] = jnp.where(evicted, moved_ref[1], vbuf[...])
    store = pltpu.make_async_copy(moved_ref, new_hbm, new_sem)
    store.start()
    for i in range(1, NXC):
        return1_wait((xc + i) % NXC)
    gate = gate_ref[pl.ds(time_ref[0], 1), :]
    for s in range(NXC):
        pack32[s, 0:BACK1, :] = recv2[s].astype(F32)
        for half in range(2):
            for h in range(HEADS):
                row = (half * HEADS + h) * TOK
                col = ((half * NXC + s) * HEADS + h) * HD
                rows = pack32[s, row : row + TOK, :] * gate[:, col : col + HD]
                out_ref[:, col : col + HD] = rows.astype(BF)

    store.wait()
    for h in range(HEADS):
        for i in (1, 2, 3):
            quad_lse(h, (seat + i) % 4).wait_send()
            for slot in range(2):
                quad_part(h, slot, (seat + i) % 4).wait_send()
        for there, k in ways:
            for each in final_copies(h, k, there):
                each.wait_send()
    step2().wait_send()
    for i in range(3):
        seat_copy(i).wait_send()
    for i in range(4):
        for k in (1, 2, 3):
            quad_query(i, (seat + k) % 4).wait_send()
    for i in range(1, NXC):
        return1((xc + i) % NXC).wait_send()
    for i in (1, 3):
        a_copy(i).wait_send()
        for h in range(HEADS):
            k_copy(h, i).wait_send()
            v_copy(h, i).wait_send()
    for part, i in ((0, 1), (1, 3)):
        src = (y + NY - i) % NY
        a_relay(src, part).wait_send()
        for h in range(HEADS):
            for each in relay_copies(src, h, part):
                each.wait_send()
    for g in range(2):
        for half in range(2):
            @pl.when(evict_target(g, half) != z)
            def _():
                evict_z(g, half).wait_send()


def attention(x, window, owner, oldest, timestep, slopes, gate_table):
    dma = pltpu.SemaphoreType.DMA
    vm = pltpu.VMEM
    in_vmem = pl.BlockSpec(memory_space=pltpu.VMEM)
    in_any = pl.BlockSpec(memory_space=pl.ANY)
    return pl.pallas_call(
        kernel,
        out_shape=(
            jax.ShapeDtypeStruct((TOK, 2 * NXC * SHARE), BF),
            jax.ShapeDtypeStruct((2, CACHE, SHARE), BF),
        ),
        in_specs=[pl.BlockSpec(memory_space=pltpu.HBM)] * 7,
        out_specs=(in_vmem, in_any),
        scratch_shapes=[
            vm((3, TOK, 2 * NXC * SHARE), BF),
            vm((CACHE, SHARE), BF),
            vm((50, 2 * NXC * SHARE), F32),
            pltpu.SMEM((NZ * NY,), jnp.int32),
            pltpu.SMEM((1,), jnp.int32),
            pltpu.SMEM((1,), jnp.int32),
            pltpu.SMEM((2 * NXC * HEADS,), F32),
            vm((2, CACHE, SHARE), BF),
            dma((10,)), dma(()),
            vm((NXC, OUT1, HD), F32),
            vm((NXC, OUT1, HD), BF),
            vm((NXC, OUT1, HD), BF),
            vm((2, 3, HALF, SHARE), F32),
            vm((NZ, ROWS, SHARE), BF),
            vm((NY, HEADS, CACHE, HD), BF),
            vm((NY, HEADS, SUMS, CACHE), BF),
            vm((NY, 2, ROWS, SHARE), BF),
            vm((HEADS, SUMS, PACK), BF),
            vm((SUMS, NZ * ROWS), F32),
            vm((8, NZ * ROWS), F32),
            vm((HEADS, 4, 2, ROWS, HD), BF),
            vm((HEADS, 4, 8, HD), F32),
            vm((HEADS, 4, 2, HD, HD), BF),
            vm((HEADS, 4, 8, HD), F32),
            vm((HEADS, 2, ROWS, HD), BF),
            vm((HEADS, 2, 8, HD), F32),
            vm((2, HEADS, 2, HD, HD), BF),
            vm((2, HEADS, 2, 8, HD), F32),
            vm((3, HALF, SHARE), BF),
            vm((NXC, BACK1, HD), BF),
            dma((NXC,)), dma((NXC,)),
            dma(()), dma(()),
            dma((3,)), dma((3,)), dma((4, 4)), dma((4, 4)),
            dma((NY, HEADS)), dma((NY, HEADS)), dma((NY, HEADS)), dma((NY, HEADS)),
            dma((2, HEADS)), dma((2, HEADS)), dma((2, HEADS)), dma((2, HEADS)),
            dma((NY,)), dma((NY,)), dma((2,)), dma((2,)),
            dma((HEADS, 2, 4)), dma((HEADS, 2, 4)), dma((HEADS, 4)), dma((HEADS, 4)),
            dma((HEADS, 3)), dma((2, HEADS, 2)), dma((HEADS, 3)), dma((2, HEADS, 2)),
            dma((2, 2)), dma((2, 2)), dma((2, NY)), dma((2, NY)),
            dma((2,)), dma((2,)),
            dma((NXC,)), dma((NXC,)), dma(()),
        ],
        compiler_params=pltpu.CompilerParams(
            collective_id=0, has_side_effects=True, vmem_limit_bytes=60 * 1024 * 1024
        ),
        cost_estimate=pl.CostEstimate(
            flops=4 * 3072 * 864 * SHARE, bytes_accessed=4 * 2**20, transcendentals=3072 * 864 * 3
        ),
    )(x, window, owner, oldest, timestep, slopes, gate_table)


def closing(attended_in, new_in, attended_out, new_out, attended, new, sem):
    parts = [(attended_in, attended, attended_out)]
    for half in range(2):
        for part in range(2):
            rows = pl.ds(part * PACK, PACK)
            parts.append(
                tuple(ref.at[half, rows, :] for ref in (new_in, new, new_out))
            )
    loads = [
        pltpu.make_async_copy(src, held, sem.at[0, i]) for i, (src, held, _) in enumerate(parts)
    ]
    stores = [
        pltpu.make_async_copy(held, dst, sem.at[1, i]) for i, (_, held, dst) in enumerate(parts)
    ]
    for load in loads:
        load.start()
    for load, store in zip(loads, stores):
        load.wait()
        store.start()
    for store in stores:
        store.wait()


def close(attended, new):
    in_hbm = pl.BlockSpec(memory_space=pltpu.HBM)
    return pl.pallas_call(
        closing,
        out_shape=tuple(jax.ShapeDtypeStruct(a.shape, a.dtype) for a in (attended, new)),
        in_specs=[in_hbm] * 2,
        out_specs=[in_hbm] * 2,
        scratch_shapes=[
            pltpu.VMEM(attended.shape, attended.dtype),
            pltpu.VMEM(new.shape, new.dtype),
            pltpu.SemaphoreType.DMA((2, 5)),
        ],
        compiler_params=pltpu.CompilerParams(vmem_limit_bytes=60 * 1024 * 1024),
    )(attended, new)


def body(active_qkv, window_kv, slot_owner, oldest_slot, timestep, time_slopes, gate_table):
    attended, new_window = attention(
        active_qkv, window_kv, slot_owner, oldest_slot, timestep, time_slopes, gate_table
    )
    return close(attended, new_window)


def solution(mesh):
    in_specs = (P(None, ("grp", "sp"), None), P(None, "grp", "sp"), P(), P(), P(), P(), P())
    out_specs = (P(("grp", "sp"), None), P(None, "grp", "sp"))
    return jax.shard_map(body, mesh=mesh, in_specs=in_specs, out_specs=out_specs, check_vma=False)
```

```python
import functools
import math

import jax
import jax.numpy as jnp
from jax import lax
from jax.experimental import pallas as pl
from jax.experimental.pallas import tpu as pltpu
from jax.sharding import PartitionSpec as P

HD = 128
WIN = 8
HEADS = 3
SHARE = HEADS * HD
TOK = 6
ROWS = 96
HALF = 48
CACHE = 768
NZ = 8
NY = 4
NXC = 8
PACK = 4 * ROWS
OUT1 = 112
BACK1 = 48
SUMS = HD + 16
LOG2E = math.log2(math.e)
COEF = LOG2E / math.sqrt(HD)
NONE = -1e30
MESH = pl.DeviceIdType.MESH
BF = jnp.bfloat16
F32 = jnp.float32
NT = (((1,), (1,)), ((), ()))


def lse2(*parts):
    top = functools.reduce(jnp.maximum, parts)
    return top + jnp.log2(sum(jnp.exp2(p - top) for p in parts))


def kernel(
    x_hbm, win_ref, owner_hbm, oldest_hbm, time_hbm, slope_hbm, gate_hbm, out_ref, new_hbm,
    x_ref, vbuf, gate_ref, owner_ref, oldest_ref, time_ref, slope_ref, moved_ref, in_sem, new_sem,
    pack32, packb, recv1, dense, qbuf, kbuf, vt, akv, vta, acc_ref, top_ref,
    so, sl, qo, ql, mo, ml, fo, fl, back, recv2,
    s1s, s1r, s2s, s2r, sas, sar, sbs, sbr, ks, kr, vs, vr, k2s, k2r, v2s, v2r, acs, acr, a2s, a2r,
    qos, qor, qls, qlr, fos, for_, fls, flr, ezs, ezr, eys, eyr, e2s, e2r, ds, dr, cp_sem,
):
    me = lax.axis_index("grp")
    sp = lax.axis_index("sp")
    z = me // NY
    y = me % NY
    zh = sp // NXC
    xc = sp % NXC
    quad = z // 4
    seat = z % 4

    def at(zz, yy):
        return {"grp": zz * NY + yy, "sp": sp}

    def beside(other):
        return {"grp": me, "sp": zh * NXC + other}

    across = {"grp": me, "sp": (1 - zh) * NXC + xc}
    over = (z + 4) % NZ
    across_over = {"grp": over * NY + y, "sp": (1 - zh) * NXC + xc}

    def copy(src, dst, send, recv, dev):
        return pltpu.make_async_remote_copy(
            src_ref=src, dst_ref=dst, send_sem=send, recv_sem=recv,
            device_id=dev, device_id_type=MESH,
        )

    def head_cols(h):
        return pl.ds(pl.multiple_of(h * HD, HD), HD)

    loads = [
        pltpu.make_async_copy(src, dst, in_sem.at[i])
        for i, (src, dst) in enumerate(
            [
                (x_hbm, x_ref), (win_ref.at[1], vbuf), (owner_hbm, owner_ref),
                (oldest_hbm, oldest_ref), (slope_hbm, slope_ref), (time_hbm, time_ref),
                (gate_hbm, gate_ref),
            ]
            + [(win_ref.at[0, :, h * HD : (h + 1) * HD], kbuf.at[y, h]) for h in range(HEADS)]
        )
    ]
    for load in loads:
        load.start()

    barrier = pltpu.get_barrier_semaphore()
    peers = [at((z + i) % NZ, y) for i in range(1, NZ)]
    peers += [at(z, (y + i) % NY) for i in range(1, NY)]
    peers += [beside((xc + i) % NXC) for i in range(1, NXC)]
    peers += [across, across_over]
    for peer in peers:
        pl.semaphore_signal(barrier, inc=1, device_id=peer, device_id_type=MESH)
    pl.semaphore_wait(barrier, len(peers))

    def k_copy(h, i):
        return copy(
            win_ref.at[0, :, h * HD : (h + 1) * HD], kbuf.at[y, h], ks.at[i, h], kr.at[i, h],
            at(z, (y + i) % NY),
        )

    def v_copy(h, i):
        return copy(
            vt.at[y, h, pl.ds(0, HD), :], vt.at[y, h, pl.ds(0, HD), :], vs.at[i, h], vr.at[i, h],
            at(z, (y + i) % NY),
        )

    def k_wait(h, i):
        src = (y + NY - i) % NY
        copy(kbuf.at[src, h], kbuf.at[src, h], ks.at[i, h], kr.at[i, h], at(z, src)).wait_recv()

    def v_wait(h, i):
        src = (y + NY - i) % NY
        rows = vt.at[src, h, pl.ds(0, HD), :]
        copy(rows, rows, vs.at[i, h], vr.at[i, h], at(z, src)).wait_recv()

    def halves(src, h, part):
        rows = pl.ds(part * PACK, PACK)
        return kbuf.at[src, h, rows, :], vt.at[src, h, pl.ds(0, HD), rows]

    def relay_copies(src, h, part):
        dev = at(z, (y + 1 + 2 * part) % NY)
        keys, values = halves(src, h, part)
        return (
            copy(keys, keys, k2s.at[part, h], k2r.at[part, h], dev),
            copy(values, values, v2s.at[part, h], v2r.at[part, h], dev),
        )

    def relay(h, keys=True, values=True):
        for part, i in ((0, 1), (1, 3)):
            on = relay_copies((y + NY - i) % NY, h, part)
            if keys:
                k_wait(h, i)
                on[0].start()
            if values:
                v_wait(h, i)
                on[1].start()

    def relay_wait(h, part):
        for each in relay_copies((y + 2) % NY, h, part):
            each.wait_recv()

    for i in (1, 3):
        k_copy(0, i).start()

    def step1(other):
        return copy(packb.at[other], recv1.at[xc], s1s.at[other], s1r.at[xc], beside(other))

    def step1_wait(other):
        copy(recv1.at[other], recv1.at[other], s1s.at[other], s1r.at[other], beside(other)).wait_recv()

    def piece(half, t, h):
        return half * 54 + (t * HEADS + h) * TOK

    loads[0].wait()
    for d in range(NXC):
        for half in range(2):
            for t in range(3):
                for h in range(HEADS):
                    col = ((half * NXC + d) * HEADS + h) * HD
                    row = piece(half, t, h)
                    pack32[d, row : row + TOK, :] = x_ref[t, :, col : col + HD].astype(F32)
        packb[d] = pack32[d].astype(BF)
    for i in range(1, NXC):
        step1((xc + i) % NXC).start()
    recv1[xc] = packb[xc]

    loads[1].wait()
    for h in range(HEADS):
        vt[y, h, 0:HD, :] = vbuf[:, h * HD : (h + 1) * HD].astype(F32).T.astype(BF)
        if h < 2:
            for i in (1, 3):
                v_copy(h, i).start()
        if h == 0:
            for i in (1, 3):
                k_copy(1, i).start()
        for src in range(NY):
            vt[src, h, HD:SUMS, :] = jnp.ones((SUMS - HD, CACHE), BF)
        vta[h, HD:SUMS, :] = jnp.ones((SUMS - HD, PACK), BF)
    for load in loads[2:]:
        load.wait()

    theirs = pl.ds(pl.multiple_of((1 - zh) * HALF, HALF), HALF)
    for h in range(HEADS):
        for i in range(4):
            qo[h, i, :, ROWS:HD, :] = jnp.zeros((2, HD - ROWS, HD), BF)
        for half in range(2):
            fo[half, h, :, ROWS:HD, :] = jnp.zeros((2, HD - ROWS, HD), BF)
            fo[half, h, :, theirs, :] = jnp.zeros((2, HALF, HD), BF)

    for i in range(1, NXC):
        step1_wait((xc + i) % NXC)
    for s in range(NXC):
        pack32[s] = recv1[s].astype(F32)
    for t in range(3):
        for s in range(NXC):
            for half in range(2):
                for h in range(HEADS):
                    row = piece(half, t, h)
                    dense[half, t, s * TOK : (s + 1) * TOK, h * HD : (h + 1) * HD] = pack32[
                        s, row : row + TOK, :
                    ]

    mine = pl.ds(pl.multiple_of(zh * HALF, HALF), HALF)

    def seat_copy(i):
        src = back.at[0] if i else qbuf.at[z, mine, :]
        dev = (at(over, y), across, across_over)[i]
        return copy(src, qbuf.at[z, mine, :], sas.at[i], sar.at[i], dev)

    def held(i):
        return qbuf.at[
            (over, z, over, z)[i], (mine, theirs, theirs, mine)[i], :
        ]

    def seat_wait(i):
        copy(held(i), held(i), sas.at[i], sar.at[i], across).wait_recv()

    def quad_query(i, other):
        return copy(
            held(i), held(i), sbs.at[i, other], sbr.at[i, seat], at(quad * 4 + other, y)
        )

    def quad_query_wait(i, other):
        block = ((1 - quad, quad, 1 - quad, quad)[i]) * 4 + other
        part = qbuf.at[block, (mine, theirs, theirs, mine)[i], :]
        copy(part, part, sbs.at[i, other], sbr.at[i, other], across).wait_recv()

    def pass_on(i):
        for k in (2, 1, 3):
            quad_query(i, (seat + k) % 4).start()

    back[0] = dense[1 - zh, 0].astype(BF)
    seat_copy(1).start()
    seat_copy(2).start()
    qbuf[z, mine, :] = dense[zh, 0].astype(BF)
    seat_copy(0).start()

    def step2():
        return copy(back.at[pl.ds(1, 2)], akv.at[y, :, mine, :], s2s, s2r, across_over)

    for t in (1, 2):
        back[t] = dense[1 - zh, t].astype(BF)
    step2().start()
    for t in (1, 2):
        akv[y, t - 1, mine, :] = dense[zh, t].astype(BF)
    pass_on(3)

    def a_copy(i):
        return copy(akv.at[y], akv.at[y], acs.at[i], acr.at[i], at(z, (y + i) % NY))

    def a_wait(i):
        src = (y + NY - i) % NY
        copy(akv.at[src], akv.at[src], acs.at[i], acr.at[i], at(z, src)).wait_recv()

    def a_relay(src, part):
        rows = akv.at[src, part]
        return copy(rows, rows, a2s.at[part], a2r.at[part], at(z, (y + 1 + 2 * part) % NY))

    def evict_rows(which, column):
        return moved_ref.at[:, pl.ds((which * NY + column) * ROWS, ROWS), :]

    def evict_part(g):
        base = pl.multiple_of(((z % 2) * NY + y) * ROWS, ROWS)
        place = (zh if g == 0 else 1 - zh) * HALF
        return (
            akv.at[y, :, theirs if g else mine, :],
            moved_ref.at[:, pl.ds(pl.multiple_of(base + place, HALF), HALF), :],
        )

    def evict_target(g, half):
        return (over if g else z) // 2 + 4 * half

    def evict_z(g, half):
        src, dst = evict_part(g)
        return copy(
            src, dst, ezs.at[g, half], ezr.at[z % 2, g], at(evict_target(g, half), y)
        )

    def evict_own(g):
        src, dst = evict_part(g)
        return pltpu.make_async_copy(src, dst, cp_sem)

    def evict_z_wait(which, g):
        group = 2 * seat + which

        @pl.when(group != (over if g else z))
        def _():
            part = akv.at[y, :, mine, :]
            copy(part, part, ezs.at[0, 0], ezr.at[which, g], across).wait_recv()

    def evict_y(which, i):
        rows = evict_rows(which, y)
        return copy(rows, rows, eys.at[which, i], eyr.at[which, i], at(z, (y + i) % NY))

    def evict_relay(which, src):
        rows = evict_rows(which, src)
        return copy(rows, rows, e2s.at[which], e2r.at[which], at(z, (y + 1 + 2 * which) % NY))

    def evict_y_wait(which, i):
        src = (y + NY - i) % NY
        rows = evict_rows(which, src)
        copy(rows, rows, eys.at[which, i], eyr.at[which, i], at(z, src)).wait_recv()

    def attend(h, active, sources, start, stop):
        cols = head_cols(h)
        q = qbuf[:, :, cols].reshape(NZ * ROWS, HD)
        slope = slope_ref[sp * HEADS + h] * LOG2E

        def window(i, part):
            src = (y + NY - i) % NY
            rows = slice(part * PACK, (part + 1) * PACK)
            slot = owner_ref[z * NY + src] - oldest_ref[0]
            age = WIN - (slot + WIN) % WIN
            return kbuf[src, h, rows, :], vt.at[src, h, :, rows], slope * age.astype(F32)

        chunks = [(akv[:, 0, :, cols].reshape(PACK, HD), vta.at[h], None)] if active else []
        chunks += [window(i, part) for i in sources for part in range(2)]
        top, acc = (None, None) if start else (top_ref[0:1, :], acc_ref[...])
        ahead = lax.dot_general(chunks[0][0], q, NT, preferred_element_type=F32)
        for n, (_, values, bias) in enumerate(chunks):
            score = ahead
            if n + 1 < len(chunks):
                ahead = lax.dot_general(chunks[n + 1][0], q, NT, preferred_element_type=F32)
            new = jnp.max(score, axis=0, keepdims=True) * COEF
            if bias is not None:
                new = new - bias
            if top is not None:
                new = jnp.maximum(top, new)
            weight = jnp.exp2(score * COEF - (new if bias is None else new + bias))
            part = jnp.dot(values[...], weight.astype(BF), preferred_element_type=F32)
            acc = part if top is None else acc * jnp.exp2(top - new) + part
            top = new
        if not stop:
            top_ref[...] = jnp.broadcast_to(top, (8, NZ * ROWS))
            acc_ref[...] = acc
            return
        total = acc[HD : HD + 1]
        mixed = acc[:HD] * (1.0 / total)
        lse = jnp.broadcast_to(top + jnp.log2(total), (8, NZ * ROWS))
        for j in range(NZ):
            pack = slice(j // 4 * PACK, (j // 4 + 1) * PACK)
            tokens, sums = mixed[:, pack], lse[:, pack]
            if j % 4:
                tokens = pltpu.roll(tokens, PACK - ROWS * (j % 4), 1)
                sums = pltpu.roll(sums, PACK - ROWS * (j % 4), 1)
            so[h, j % 4, j // 4] = tokens[:, :HD].T[:ROWS].astype(BF)
            sl[h, j % 4, 4 * (j // 4) : 4 * (j // 4) + 4, :] = sums[:4, :HD]

    def quad_lse(h, other):
        return copy(
            sl.at[h, other], ql.at[h, seat], qls.at[h, other], qlr.at[h, seat],
            at(quad * 4 + other, y),
        )

    def quad_part(h, slot, other):
        return copy(
            so.at[h, other, slot], qo.at[h, seat, slot, pl.ds(0, ROWS), :],
            qos.at[h, slot, other], qor.at[h, slot, seat], at(quad * 4 + other, y),
        )

    def quad_wait(h, slot, other):
        part = qo.at[h, other, slot, pl.ds(0, ROWS), :]
        copy(part, part, qos.at[h, slot, other], qor.at[h, slot, other], across).wait_recv()

    def quad_lse_wait(h, other):
        part = ql.at[h, other]
        copy(part, part, qls.at[h, other], qlr.at[h, other], across).wait_recv()

    def to_quad(h):
        for i in (2, 1, 3):
            quad_lse(h, (seat + i) % 4).start()
        for slot in (quad, 1 - quad):
            for i in (2, 1, 3):
                quad_part(h, slot, (seat + i) % 4).start()
        ql[h, seat] = sl[h, seat]
        qo[h, seat, :, 0:ROWS, :] = so[h, seat]

    def spread(weight, first_row, rows):
        at_row = lax.broadcasted_iota(jnp.int32, (rows, HD), 0) + first_row
        at_col = lax.broadcasted_iota(jnp.int32, (rows, HD), 1)
        return jnp.where(at_row == at_col, weight, 0.0).astype(BF)

    def final_copies(h, k, there):
        dev = (at(over, y), across, across_over)[there]
        rows = theirs if there else mine
        return (
            copy(ml.at[h, k], fl.at[zh, h, quad], fls.at[h, there], flr.at[zh, h, quad], dev),
            copy(
                mo.at[h, k, rows, :], fo.at[zh, h, quad, rows, :], fos.at[h, there],
                for_.at[zh, h, quad], dev,
            ),
        )

    ways = ((2, 1), (1, 0), (0, 1))

    def reduce(h):
        for i in (1, 3, 2):
            quad_lse_wait(h, (seat + i) % 4)
        for k in (0, 1):
            slot = (quad + k) % 2
            for i in (1, 3, 2):
                quad_wait(h, slot, (seat + i) % 4)
            row = pl.ds(slot * 4, 1)
            parts = [ql[h, i, row, :] for i in range(4)]
            whole = lse2(*parts)
            weights = jnp.concatenate(
                [spread(jnp.exp2(p - whole), 0, ROWS) for p in parts], axis=1
            )
            mo[h, k] = jnp.dot(
                weights, qo[h, :, slot].reshape(4 * HD, HD), preferred_element_type=F32
            ).astype(BF)
            ml[h, k] = jnp.broadcast_to(whole, (8, HD))
            for there, which in ways:
                if which == k:
                    for each in final_copies(h, k, there):
                        each.start()
        fl[zh, h, quad] = ml[h, 0]
        fo[zh, h, quad, mine, :] = mo[h, 0, mine, :]

    def final_wait(half, h, which):
        part = fl.at[half, h, which]
        copy(part, part, fls.at[h, 0], flr.at[half, h, which], across).wait_recv()
        part = fo.at[half, h, which, mine, :]
        copy(part, part, fos.at[h, 0], for_.at[half, h, which], across).wait_recv()

    def finish(h):
        final_wait(zh, h, 1 - quad)
        final_wait(1 - zh, h, 0)
        final_wait(1 - zh, h, 1)
        for half in range(2):
            parts = [fl[half, h, i, 0:1, :] for i in range(2)]
            whole = lse2(*parts)
            weights = jnp.concatenate(
                [spread(jnp.exp2(p - whole), zh * HALF, HALF) for p in parts], axis=1
            )
            dense[half, 0, :, h * HD : (h + 1) * HD] = jnp.dot(
                weights, fo[half, h].reshape(2 * HD, HD), preferred_element_type=F32
            )

    seat_wait(0)
    pass_on(0)
    seat_wait(2)
    pass_on(2)
    relay(0)
    seat_wait(1)
    pass_on(1)
    for i in (1, 3):
        k_copy(2, i).start()
    part = akv.at[y, :, theirs, :]
    copy(part, part, s2s, s2r, across).wait_recv()
    for i in (1, 3):
        a_copy(i).start()
    for g in range(2):
        for half in range(2):
            @pl.when(evict_target(g, half) != z)
            def _():
                evict_z(g, half).start()

            @pl.when(evict_target(g, half) == z)
            def _():
                evict_own(g).start()

    relay(1)
    for part, i in ((0, 1), (1, 3)):
        a_wait(i)
        a_relay((y + NY - i) % NY, part).start()
    for i in (1, 3):
        v_copy(2, i).start()
    for i in (3, 0, 2, 1):
        for k in (1, 2, 3):
            quad_query_wait(i, (seat + k) % 4)

    for part in range(2):
        relay_wait(0, part)
    attend(0, False, (0, 1, 3, 2), True, False)
    for part in range(2):
        a_relay((y + 2) % NY, part).wait_recv()
    for h in range(HEADS):
        values = akv[:, 1, :, h * HD : (h + 1) * HD].reshape(PACK, HD)
        vta[h, 0:HD, :] = values.astype(F32).T.astype(BF)
    attend(0, True, (), False, True)
    to_quad(0)
    relay(2, values=False)
    for part in range(2):
        relay_wait(1, part)
    attend(1, True, (0, 1, 3, 2), True, True)
    to_quad(1)
    relay(2, keys=False)
    attend(2, True, (0, 1, 3), True, False)
    for part in range(2):
        relay_wait(2, part)
    attend(2, False, (2,), False, True)
    to_quad(2)
    reduce(0)
    reduce(1)

    for which in range(2):
        for g in range(2):
            evict_z_wait(which, g)

    for g in range(2):
        for half in range(2):
            @pl.when(evict_target(g, half) == z)
            def _():
                evict_own(g).wait()

    for which in range(2):
        for i in (1, 3):
            evict_y(which, i).start()

    reduce(2)
    finish(0)
    finish(1)
    for which, i in ((0, 1), (1, 3)):
        evict_y_wait(which, i)
        evict_relay(which, (y + NY - i) % NY).start()
    finish(2)

    def return1(other):
        return copy(
            packb.at[other, pl.ds(0, BACK1), :], recv2.at[xc], ds.at[other], dr.at[xc],
            beside(other),
        )

    def return1_wait(other):
        part = recv2.at[other]
        copy(part, part, ds.at[other], dr.at[other], beside(other)).wait_recv()

    for i in range(1, NXC):
        step1((xc + i) % NXC).wait_send()
    for d in range(NXC):
        for half in range(2):
            for h in range(HEADS):
                row = (half * HEADS + h) * TOK
                pack32[d, row : row + TOK, :] = dense[
                    half, 0, d * TOK : (d + 1) * TOK, h * HD : (h + 1) * HD
                ]
        packb[d, 0:BACK1, :] = pack32[d, 0:BACK1, :].astype(BF)
    for i in range(1, NXC):
        return1((xc + i) % NXC).start()
    recv2[xc] = packb[xc, 0:BACK1, :]
    evict_y_wait(1, 1)
    evict_y_wait(0, 3)
    for which in range(2):
        evict_relay(which, (y + 2) % NY).wait_recv()
    for which, i in ((0, 1), (1, 3)):
        evict_relay(which, (y + NY - i) % NY).wait_send()
        for side in (1, 3):
            evict_y(which, side).wait_send()
    evicted = owner_ref[me] == oldest_ref[0]
    for h in range(HEADS):
        cols = slice(h * HD, (h + 1) * HD)
        moved_ref[0, :, cols] = jnp.where(evicted, moved_ref[0, :, cols], kbuf[y, h])
    moved_ref[1] = jnp.where(evicted, moved_ref[1], vbuf[...])
    store = pltpu.make_async_copy(moved_ref, new_hbm, new_sem)
    store.start()
    for i in range(1, NXC):
        return1_wait((xc + i) % NXC)
    gate = gate_ref[pl.ds(time_ref[0], 1), :]
    for s in range(NXC):
        pack32[s, 0:BACK1, :] = recv2[s].astype(F32)
        for half in range(2):
            for h in range(HEADS):
                row = (half * HEADS + h) * TOK
                col = ((half * NXC + s) * HEADS + h) * HD
                rows = pack32[s, row : row + TOK, :] * gate[:, col : col + HD]
                out_ref[:, col : col + HD] = rows.astype(BF)

    store.wait()
    for h in range(HEADS):
        for i in (1, 2, 3):
            quad_lse(h, (seat + i) % 4).wait_send()
            for slot in range(2):
                quad_part(h, slot, (seat + i) % 4).wait_send()
        for there, k in ways:
            for each in final_copies(h, k, there):
                each.wait_send()
    step2().wait_send()
    for i in range(3):
        seat_copy(i).wait_send()
    for i in range(4):
        for k in (1, 2, 3):
            quad_query(i, (seat + k) % 4).wait_send()
    for i in range(1, NXC):
        return1((xc + i) % NXC).wait_send()
    for i in (1, 3):
        a_copy(i).wait_send()
        for h in range(HEADS):
            k_copy(h, i).wait_send()
            v_copy(h, i).wait_send()
    for part, i in ((0, 1), (1, 3)):
        src = (y + NY - i) % NY
        a_relay(src, part).wait_send()
        for h in range(HEADS):
            for each in relay_copies(src, h, part):
                each.wait_send()
    for g in range(2):
        for half in range(2):
            @pl.when(evict_target(g, half) != z)
            def _():
                evict_z(g, half).wait_send()


def attention(x, window, owner, oldest, timestep, slopes, gate_table):
    dma = pltpu.SemaphoreType.DMA
    vm = pltpu.VMEM
    in_vmem = pl.BlockSpec(memory_space=pltpu.VMEM)
    in_any = pl.BlockSpec(memory_space=pl.ANY)
    return pl.pallas_call(
        kernel,
        out_shape=(
            jax.ShapeDtypeStruct((TOK, 2 * NXC * SHARE), BF),
            jax.ShapeDtypeStruct((2, CACHE, SHARE), BF),
        ),
        in_specs=[pl.BlockSpec(memory_space=pltpu.HBM)] * 7,
        out_specs=(in_vmem, in_any),
        scratch_shapes=[
            vm((3, TOK, 2 * NXC * SHARE), BF),
            vm((CACHE, SHARE), BF),
            vm((50, 2 * NXC * SHARE), F32),
            pltpu.SMEM((NZ * NY,), jnp.int32),
            pltpu.SMEM((1,), jnp.int32),
            pltpu.SMEM((1,), jnp.int32),
            pltpu.SMEM((2 * NXC * HEADS,), F32),
            vm((2, CACHE, SHARE), BF),
            dma((10,)), dma(()),
            vm((NXC, OUT1, HD), F32),
            vm((NXC, OUT1, HD), BF),
            vm((NXC, OUT1, HD), BF),
            vm((2, 3, HALF, SHARE), F32),
            vm((NZ, ROWS, SHARE), BF),
            vm((NY, HEADS, CACHE, HD), BF),
            vm((NY, HEADS, SUMS, CACHE), BF),
            vm((NY, 2, ROWS, SHARE), BF),
            vm((HEADS, SUMS, PACK), BF),
            vm((SUMS, NZ * ROWS), F32),
            vm((8, NZ * ROWS), F32),
            vm((HEADS, 4, 2, ROWS, HD), BF),
            vm((HEADS, 4, 8, HD), F32),
            vm((HEADS, 4, 2, HD, HD), BF),
            vm((HEADS, 4, 8, HD), F32),
            vm((HEADS, 2, ROWS, HD), BF),
            vm((HEADS, 2, 8, HD), F32),
            vm((2, HEADS, 2, HD, HD), BF),
            vm((2, HEADS, 2, 8, HD), F32),
            vm((3, HALF, SHARE), BF),
            vm((NXC, BACK1, HD), BF),
            dma((NXC,)), dma((NXC,)),
            dma(()), dma(()),
            dma((3,)), dma((3,)), dma((4, 4)), dma((4, 4)),
            dma((NY, HEADS)), dma((NY, HEADS)), dma((NY, HEADS)), dma((NY, HEADS)),
            dma((2, HEADS)), dma((2, HEADS)), dma((2, HEADS)), dma((2, HEADS)),
            dma((NY,)), dma((NY,)), dma((2,)), dma((2,)),
            dma((HEADS, 2, 4)), dma((HEADS, 2, 4)), dma((HEADS, 4)), dma((HEADS, 4)),
            dma((HEADS, 3)), dma((2, HEADS, 2)), dma((HEADS, 3)), dma((2, HEADS, 2)),
            dma((2, 2)), dma((2, 2)), dma((2, NY)), dma((2, NY)),
            dma((2,)), dma((2,)),
            dma((NXC,)), dma((NXC,)), dma(()),
        ],
        compiler_params=pltpu.CompilerParams(
            collective_id=0, has_side_effects=True, vmem_limit_bytes=60 * 1024 * 1024
        ),
        cost_estimate=pl.CostEstimate(
            flops=4 * 3072 * 864 * SHARE, bytes_accessed=4 * 2**20, transcendentals=3072 * 864 * 3
        ),
    )(x, window, owner, oldest, timestep, slopes, gate_table)


def closing(attended_in, new_in, attended_out, new_out, attended, new, sem):
    parts = [(attended_in, attended, attended_out)]
    for half in range(2):
        for part in range(2):
            rows = pl.ds(part * PACK, PACK)
            parts.append(
                tuple(ref.at[half, rows, :] for ref in (new_in, new, new_out))
            )
    loads = [
        pltpu.make_async_copy(src, held, sem.at[0, i]) for i, (src, held, _) in enumerate(parts)
    ]
    stores = [
        pltpu.make_async_copy(held, dst, sem.at[1, i]) for i, (_, held, dst) in enumerate(parts)
    ]
    for load in loads:
        load.start()
    for load, store in zip(loads, stores):
        load.wait()
        store.start()
    for store in stores:
        store.wait()


def close(attended, new):
    in_hbm = pl.BlockSpec(memory_space=pltpu.HBM)
    return pl.pallas_call(
        closing,
        out_shape=tuple(jax.ShapeDtypeStruct(a.shape, a.dtype) for a in (attended, new)),
        in_specs=[in_hbm] * 2,
        out_specs=[in_hbm] * 2,
        scratch_shapes=[
            pltpu.VMEM(attended.shape, attended.dtype),
            pltpu.VMEM(new.shape, new.dtype),
            pltpu.SemaphoreType.DMA((2, 5)),
        ],
        compiler_params=pltpu.CompilerParams(vmem_limit_bytes=60 * 1024 * 1024),
    )(attended, new)


def body(active_qkv, window_kv, slot_owner, oldest_slot, timestep, time_slopes, gate_table):
    attended, new_window = attention(
        active_qkv, window_kv, slot_owner, oldest_slot, timestep, time_slopes, gate_table
    )
    return close(attended, new_window)


def solution(mesh):
    in_specs = (P(None, ("grp", "sp"), None), P(None, "grp", "sp"), P(), P(), P(), P(), P())
    out_specs = (P(("grp", "sp"), None), P(None, "grp", "sp"))
    return jax.shard_map(body, mesh=mesh, in_specs=in_specs, out_specs=out_specs, check_vma=False)
```

```python
import functools
import math

import jax
import jax.numpy as jnp
from jax import lax
from jax.experimental import pallas as pl
from jax.experimental.pallas import tpu as pltpu
from jax.sharding import PartitionSpec as P

HD = 128
WIN = 8
HEADS = 3
SHARE = HEADS * HD
TOK = 6
ROWS = 96
HALF = 48
CACHE = 768
NZ = 8
NY = 4
NXC = 8
PACK = 4 * ROWS
OUT1 = 112
BACK1 = 48
SUMS = HD + 16
LOG2E = math.log2(math.e)
COEF = LOG2E / math.sqrt(HD)
NONE = -1e30
MESH = pl.DeviceIdType.MESH
BF = jnp.bfloat16
F32 = jnp.float32
NT = (((1,), (1,)), ((), ()))


def lse2(*parts):
    top = functools.reduce(jnp.maximum, parts)
    return top + jnp.log2(sum(jnp.exp2(p - top) for p in parts))


def kernel(
    x_hbm, win_ref, owner_hbm, oldest_hbm, time_hbm, slope_hbm, gate_hbm, out_ref, new_hbm,
    x_ref, vbuf, gate_ref, owner_ref, oldest_ref, time_ref, slope_ref, moved_ref, in_sem, new_sem,
    pack32, packb, recv1, dense, qbuf, kbuf, vt, akv, vta, acc_ref, top_ref,
    so, sl, qo, ql, mo, ml, fo, fl, back, recv2,
    s1s, s1r, s2s, s2r, sas, sar, sbs, sbr, ks, kr, vs, vr, k2s, k2r, v2s, v2r, acs, acr, a2s, a2r,
    qos, qor, qls, qlr, fos, for_, fls, flr, ezs, ezr, eys, eyr, e2s, e2r, ds, dr, cp_sem,
):
    me = lax.axis_index("grp")
    sp = lax.axis_index("sp")
    z = me // NY
    y = me % NY
    zh = sp // NXC
    xc = sp % NXC
    quad = z // 4
    seat = z % 4

    def at(zz, yy):
        return {"grp": zz * NY + yy, "sp": sp}

    def beside(other):
        return {"grp": me, "sp": zh * NXC + other}

    across = {"grp": me, "sp": (1 - zh) * NXC + xc}
    over = (z + 4) % NZ
    across_over = {"grp": over * NY + y, "sp": (1 - zh) * NXC + xc}

    def copy(src, dst, send, recv, dev):
        return pltpu.make_async_remote_copy(
            src_ref=src, dst_ref=dst, send_sem=send, recv_sem=recv,
            device_id=dev, device_id_type=MESH,
        )

    def head_cols(h):
        return pl.ds(pl.multiple_of(h * HD, HD), HD)

    loads = [
        pltpu.make_async_copy(src, dst, in_sem.at[i])
        for i, (src, dst) in enumerate(
            [
                (x_hbm, x_ref), (win_ref.at[1], vbuf), (owner_hbm, owner_ref),
                (oldest_hbm, oldest_ref), (slope_hbm, slope_ref), (time_hbm, time_ref),
                (gate_hbm, gate_ref),
            ]
            + [(win_ref.at[0, :, h * HD : (h + 1) * HD], kbuf.at[y, h]) for h in range(HEADS)]
        )
    ]
    for load in loads:
        load.start()

    barrier = pltpu.get_barrier_semaphore()
    peers = [at((z + i) % NZ, y) for i in range(1, NZ)]
    peers += [at(z, (y + i) % NY) for i in range(1, NY)]
    peers += [beside((xc + i) % NXC) for i in range(1, NXC)]
    peers += [across, across_over]
    for peer in peers:
        pl.semaphore_signal(barrier, inc=1, device_id=peer, device_id_type=MESH)
    pl.semaphore_wait(barrier, len(peers))

    def k_copy(h, i):
        return copy(
            win_ref.at[0, :, h * HD : (h + 1) * HD], kbuf.at[y, h], ks.at[i, h], kr.at[i, h],
            at(z, (y + i) % NY),
        )

    def v_copy(h, i):
        return copy(
            vt.at[y, h, pl.ds(0, HD), :], vt.at[y, h, pl.ds(0, HD), :], vs.at[i, h], vr.at[i, h],
            at(z, (y + i) % NY),
        )

    def k_wait(h, i):
        src = (y + NY - i) % NY
        copy(kbuf.at[src, h], kbuf.at[src, h], ks.at[i, h], kr.at[i, h], at(z, src)).wait_recv()

    def v_wait(h, i):
        src = (y + NY - i) % NY
        rows = vt.at[src, h, pl.ds(0, HD), :]
        copy(rows, rows, vs.at[i, h], vr.at[i, h], at(z, src)).wait_recv()

    def halves(src, h, part):
        rows = pl.ds(part * PACK, PACK)
        return kbuf.at[src, h, rows, :], vt.at[src, h, pl.ds(0, HD), rows]

    def relay_copies(src, h, part):
        dev = at(z, (y + 1 + 2 * part) % NY)
        keys, values = halves(src, h, part)
        return (
            copy(keys, keys, k2s.at[part, h], k2r.at[part, h], dev),
            copy(values, values, v2s.at[part, h], v2r.at[part, h], dev),
        )

    def relay(h, keys=True, values=True):
        for part, i in ((0, 1), (1, 3)):
            on = relay_copies((y + NY - i) % NY, h, part)
            if keys:
                k_wait(h, i)
                on[0].start()
            if values:
                v_wait(h, i)
                on[1].start()

    def relay_wait(h, part):
        for each in relay_copies((y + 2) % NY, h, part):
            each.wait_recv()

    for i in (1, 3):
        k_copy(0, i).start()

    def step1(other):
        return copy(packb.at[other], recv1.at[xc], s1s.at[other], s1r.at[xc], beside(other))

    def step1_wait(other):
        copy(recv1.at[other], recv1.at[other], s1s.at[other], s1r.at[other], beside(other)).wait_recv()

    def piece(half, t, h):
        return half * 54 + (t * HEADS + h) * TOK

    loads[0].wait()
    for d in range(NXC):
        for half in range(2):
            for t in range(3):
                for h in range(HEADS):
                    col = ((half * NXC + d) * HEADS + h) * HD
                    row = piece(half, t, h)
                    pack32[d, row : row + TOK, :] = x_ref[t, :, col : col + HD].astype(F32)
        packb[d] = pack32[d].astype(BF)
    for i in range(1, NXC):
        step1((xc + i) % NXC).start()
    recv1[xc] = packb[xc]

    loads[1].wait()
    for h in range(HEADS):
        vt[y, h, 0:HD, :] = vbuf[:, h * HD : (h + 1) * HD].astype(F32).T.astype(BF)
        if h < 2:
            for i in (1, 3):
                v_copy(h, i).start()
        if h == 0:
            for i in (1, 3):
                k_copy(1, i).start()
        for src in range(NY):
            vt[src, h, HD:SUMS, :] = jnp.ones((SUMS - HD, CACHE), BF)
        vta[h, HD:SUMS, :] = jnp.ones((SUMS - HD, PACK), BF)
    for load in loads[2:]:
        load.wait()

    theirs = pl.ds(pl.multiple_of((1 - zh) * HALF, HALF), HALF)
    for h in range(HEADS):
        for i in range(4):
            qo[h, i, :, ROWS:HD, :] = jnp.zeros((2, HD - ROWS, HD), BF)
        for half in range(2):
            fo[half, h, :, ROWS:HD, :] = jnp.zeros((2, HD - ROWS, HD), BF)
            fo[half, h, :, theirs, :] = jnp.zeros((2, HALF, HD), BF)

    for i in range(1, NXC):
        step1_wait((xc + i) % NXC)
    for s in range(NXC):
        pack32[s] = recv1[s].astype(F32)
    for t in range(3):
        for s in range(NXC):
            for half in range(2):
                for h in range(HEADS):
                    row = piece(half, t, h)
                    dense[half, t, s * TOK : (s + 1) * TOK, h * HD : (h + 1) * HD] = pack32[
                        s, row : row + TOK, :
                    ]

    mine = pl.ds(pl.multiple_of(zh * HALF, HALF), HALF)

    def seat_copy(i):
        src = back.at[0] if i else qbuf.at[z, mine, :]
        dev = (at(over, y), across, across_over)[i]
        return copy(src, qbuf.at[z, mine, :], sas.at[i], sar.at[i], dev)

    def held(i):
        return qbuf.at[
            (over, z, over, z)[i], (mine, theirs, theirs, mine)[i], :
        ]

    def seat_wait(i):
        copy(held(i), held(i), sas.at[i], sar.at[i], across).wait_recv()

    def quad_query(i, other):
        return copy(
            held(i), held(i), sbs.at[i, other], sbr.at[i, seat], at(quad * 4 + other, y)
        )

    def quad_query_wait(i, other):
        block = ((1 - quad, quad, 1 - quad, quad)[i]) * 4 + other
        part = qbuf.at[block, (mine, theirs, theirs, mine)[i], :]
        copy(part, part, sbs.at[i, other], sbr.at[i, other], across).wait_recv()

    def pass_on(i):
        for k in (2, 1, 3):
            quad_query(i, (seat + k) % 4).start()

    back[0] = dense[1 - zh, 0, 0:HALF].astype(BF)
    seat_copy(1).start()
    seat_copy(2).start()
    qbuf[z, mine, :] = dense[zh, 0, 0:HALF].astype(BF)
    seat_copy(0).start()

    def step2():
        return copy(back.at[pl.ds(1, 2)], akv.at[y, :, mine, :], s2s, s2r, across_over)

    for t in (1, 2):
        back[t] = dense[1 - zh, t, 0:HALF].astype(BF)
    step2().start()
    for t in (1, 2):
        akv[y, t - 1, mine, :] = dense[zh, t, 0:HALF].astype(BF)
    pass_on(3)

    def a_copy(i):
        return copy(akv.at[y], akv.at[y], acs.at[i], acr.at[i], at(z, (y + i) % NY))

    def a_wait(i):
        src = (y + NY - i) % NY
        copy(akv.at[src], akv.at[src], acs.at[i], acr.at[i], at(z, src)).wait_recv()

    def a_relay(src, part):
        rows = akv.at[src, part]
        return copy(rows, rows, a2s.at[part], a2r.at[part], at(z, (y + 1 + 2 * part) % NY))

    def evict_rows(which, column):
        return moved_ref.at[:, pl.ds((which * NY + column) * ROWS, ROWS), :]

    def evict_part(g):
        base = pl.multiple_of(((z % 2) * NY + y) * ROWS, ROWS)
        place = (zh if g == 0 else 1 - zh) * HALF
        return (
            akv.at[y, :, theirs if g else mine, :],
            moved_ref.at[:, pl.ds(pl.multiple_of(base + place, HALF), HALF), :],
        )

    def evict_target(g, half):
        return (over if g else z) // 2 + 4 * half

    def evict_z(g, half):
        src, dst = evict_part(g)
        return copy(
            src, dst, ezs.at[g, half], ezr.at[z % 2, g], at(evict_target(g, half), y)
        )

    def evict_own(g):
        src, dst = evict_part(g)
        return pltpu.make_async_copy(src, dst, cp_sem)

    def evict_z_wait(which, g):
        group = 2 * seat + which

        @pl.when(group != (over if g else z))
        def _():
            part = akv.at[y, :, mine, :]
            copy(part, part, ezs.at[0, 0], ezr.at[which, g], across).wait_recv()

    def evict_y(which, i):
        rows = evict_rows(which, y)
        return copy(rows, rows, eys.at[which, i], eyr.at[which, i], at(z, (y + i) % NY))

    def evict_relay(which, src):
        rows = evict_rows(which, src)
        return copy(rows, rows, e2s.at[which], e2r.at[which], at(z, (y + 1 + 2 * which) % NY))

    def evict_y_wait(which, i):
        src = (y + NY - i) % NY
        rows = evict_rows(which, src)
        copy(rows, rows, eys.at[which, i], eyr.at[which, i], at(z, src)).wait_recv()

    def attend(h, active, sources, start, stop):
        cols = head_cols(h)
        q = qbuf[:, :, cols].reshape(NZ * ROWS, HD)
        slope = slope_ref[sp * HEADS + h] * LOG2E

        def window(i, part):
            src = (y + NY - i) % NY
            rows = slice(part * PACK, (part + 1) * PACK)
            slot = owner_ref[z * NY + src] - oldest_ref[0]
            age = WIN - (slot + WIN) % WIN
            return kbuf[src, h, rows, :], vt.at[src, h, :, rows], slope * age.astype(F32)

        chunks = [(akv[:, 0, :, cols].reshape(PACK, HD), vta.at[h], None)] if active else []
        chunks += [window(i, part) for i in sources for part in range(2)]
        top, acc = (None, None) if start else (top_ref[0:1, :], acc_ref[...])
        ahead = lax.dot_general(chunks[0][0], q, NT, preferred_element_type=F32)
        for n, (_, values, bias) in enumerate(chunks):
            score = ahead
            if n + 1 < len(chunks):
                ahead = lax.dot_general(chunks[n + 1][0], q, NT, preferred_element_type=F32)
            new = jnp.max(score, axis=0, keepdims=True) * COEF
            if bias is not None:
                new = new - bias
            if top is not None:
                new = jnp.maximum(top, new)
            weight = jnp.exp2(score * COEF - (new if bias is None else new + bias))
            part = jnp.dot(values[...], weight.astype(BF), preferred_element_type=F32)
            acc = part if top is None else acc * jnp.exp2(top - new) + part
            top = new
        if not stop:
            top_ref[...] = jnp.broadcast_to(top, (8, NZ * ROWS))
            acc_ref[...] = acc
            return
        total = acc[HD : HD + 1]
        mixed = acc[:HD] * (1.0 / total)
        lse = jnp.broadcast_to(top + jnp.log2(total), (8, NZ * ROWS))
        for j in range(NZ):
            pack = slice(j // 4 * PACK, (j // 4 + 1) * PACK)
            tokens, sums = mixed[:, pack], lse[:, pack]
            if j % 4:
                tokens = pltpu.roll(tokens, PACK - ROWS * (j % 4), 1)
                sums = pltpu.roll(sums, PACK - ROWS * (j % 4), 1)
            so[h, j % 4, j // 4] = tokens[:, :HD].T[:ROWS].astype(BF)
            sl[h, j % 4, 4 * (j // 4) : 4 * (j // 4) + 4, :] = sums[:4, :HD]

    def quad_lse(h, other):
        return copy(
            sl.at[h, other], ql.at[h, seat], qls.at[h, other], qlr.at[h, seat],
            at(quad * 4 + other, y),
        )

    def quad_part(h, slot, other):
        return copy(
            so.at[h, other, slot], qo.at[h, seat, slot, pl.ds(0, ROWS), :],
            qos.at[h, slot, other], qor.at[h, slot, seat], at(quad * 4 + other, y),
        )

    def quad_wait(h, slot, other):
        part = qo.at[h, other, slot, pl.ds(0, ROWS), :]
        copy(part, part, qos.at[h, slot, other], qor.at[h, slot, other], across).wait_recv()

    def quad_lse_wait(h, other):
        part = ql.at[h, other]
        copy(part, part, qls.at[h, other], qlr.at[h, other], across).wait_recv()

    def to_quad(h):
        for i in (2, 1, 3):
            quad_lse(h, (seat + i) % 4).start()
        for slot in (quad, 1 - quad):
            for i in (2, 1, 3):
                quad_part(h, slot, (seat + i) % 4).start()
        ql[h, seat] = sl[h, seat]
        qo[h, seat, :, 0:ROWS, :] = so[h, seat]

    def spread(weight, first_row, rows):
        at_row = lax.broadcasted_iota(jnp.int32, (rows, HD), 0) + first_row
        at_col = lax.broadcasted_iota(jnp.int32, (rows, HD), 1)
        return jnp.where(at_row == at_col, weight, 0.0).astype(BF)

    def final_copies(h, k, there):
        dev = (at(over, y), across, across_over)[there]
        rows = theirs if there else mine
        return (
            copy(ml.at[h, k], fl.at[zh, h, quad], fls.at[h, there], flr.at[zh, h, quad], dev),
            copy(
                mo.at[h, k, rows, :], fo.at[zh, h, quad, rows, :], fos.at[h, there],
                for_.at[zh, h, quad], dev,
            ),
        )

    ways = ((2, 1), (1, 0), (0, 1))

    def reduce(h):
        for i in (1, 3, 2):
            quad_lse_wait(h, (seat + i) % 4)
        for k in (0, 1):
            slot = (quad + k) % 2
            for i in (1, 3, 2):
                quad_wait(h, slot, (seat + i) % 4)
            row = pl.ds(slot * 4, 1)
            parts = [ql[h, i, row, :] for i in range(4)]
            whole = lse2(*parts)
            weights = jnp.concatenate(
                [spread(jnp.exp2(p - whole), 0, ROWS) for p in parts], axis=1
            )
            mo[h, k] = jnp.dot(
                weights, qo[h, :, slot].reshape(4 * HD, HD), preferred_element_type=F32
            ).astype(BF)
            ml[h, k] = jnp.broadcast_to(whole, (8, HD))
            for there, which in ways:
                if which == k:
                    for each in final_copies(h, k, there):
                        each.start()
        fl[zh, h, quad] = ml[h, 0]
        fo[zh, h, quad, mine, :] = mo[h, 0, mine, :]

    def final_wait(half, h, which):
        part = fl.at[half, h, which]
        copy(part, part, fls.at[h, 0], flr.at[half, h, which], across).wait_recv()
        part = fo.at[half, h, which, mine, :]
        copy(part, part, fos.at[h, 0], for_.at[half, h, which], across).wait_recv()

    def finish(h):
        final_wait(zh, h, 1 - quad)
        final_wait(1 - zh, h, 0)
        final_wait(1 - zh, h, 1)
        for half in range(2):
            parts = [fl[half, h, i, 0:1, :] for i in range(2)]
            whole = lse2(*parts)
            weights = jnp.concatenate(
                [spread(jnp.exp2(p - whole), zh * HALF, HALF) for p in parts], axis=1
            )
            dense[half, 0, 0:HALF, h * HD : (h + 1) * HD] = jnp.dot(
                weights, fo[half, h].reshape(2 * HD, HD), preferred_element_type=F32
            )

    seat_wait(0)
    pass_on(0)
    seat_wait(2)
    pass_on(2)
    relay(0)
    seat_wait(1)
    pass_on(1)
    for i in (1, 3):
        k_copy(2, i).start()
    part = akv.at[y, :, theirs, :]
    copy(part, part, s2s, s2r, across).wait_recv()
    for i in (1, 3):
        a_copy(i).start()
    for g in range(2):
        for half in range(2):
            @pl.when(evict_target(g, half) != z)
            def _():
                evict_z(g, half).start()

            @pl.when(evict_target(g, half) == z)
            def _():
                evict_own(g).start()

    relay(1)
    for part, i in ((0, 1), (1, 3)):
        a_wait(i)
        a_relay((y + NY - i) % NY, part).start()
    for i in (1, 3):
        v_copy(2, i).start()
    for i in (3, 0, 2, 1):
        for k in (1, 2, 3):
            quad_query_wait(i, (seat + k) % 4)

    for part in range(2):
        relay_wait(0, part)
    attend(0, False, (0, 1, 3, 2), True, False)
    for part in range(2):
        a_relay((y + 2) % NY, part).wait_recv()
    for h in range(HEADS):
        values = akv[:, 1, :, h * HD : (h + 1) * HD].reshape(PACK, HD)
        vta[h, 0:HD, :] = values.astype(F32).T.astype(BF)
    attend(0, True, (), False, True)
    to_quad(0)
    relay(2, values=False)
    for part in range(2):
        relay_wait(1, part)
    attend(1, True, (0, 1, 3, 2), True, True)
    to_quad(1)
    relay(2, keys=False)
    attend(2, True, (0, 1, 3), True, False)
    for part in range(2):
        relay_wait(2, part)
    attend(2, False, (2,), False, True)
    to_quad(2)
    reduce(0)
    reduce(1)

    for which in range(2):
        for g in range(2):
            evict_z_wait(which, g)

    for g in range(2):
        for half in range(2):
            @pl.when(evict_target(g, half) == z)
            def _():
                evict_own(g).wait()

    for which in range(2):
        for i in (1, 3):
            evict_y(which, i).start()

    reduce(2)
    finish(0)
    finish(1)
    for which, i in ((0, 1), (1, 3)):
        evict_y_wait(which, i)
        evict_relay(which, (y + NY - i) % NY).start()
    finish(2)

    def return1(other):
        return copy(
            packb.at[other, pl.ds(0, BACK1), :], recv2.at[xc], ds.at[other], dr.at[xc],
            beside(other),
        )

    def return1_wait(other):
        part = recv2.at[other]
        copy(part, part, ds.at[other], dr.at[other], beside(other)).wait_recv()

    for i in range(1, NXC):
        step1((xc + i) % NXC).wait_send()
    for d in range(NXC):
        for half in range(2):
            for h in range(HEADS):
                row = (half * HEADS + h) * TOK
                pack32[d, row : row + TOK, :] = dense[
                    half, 0, d * TOK : (d + 1) * TOK, h * HD : (h + 1) * HD
                ]
        packb[d, 0:BACK1, :] = pack32[d, 0:BACK1, :].astype(BF)
    for i in range(1, NXC):
        return1((xc + i) % NXC).start()
    recv2[xc] = packb[xc, 0:BACK1, :]
    evict_y_wait(1, 1)
    evict_y_wait(0, 3)
    for which in range(2):
        evict_relay(which, (y + 2) % NY).wait_recv()
    for which, i in ((0, 1), (1, 3)):
        evict_relay(which, (y + NY - i) % NY).wait_send()
        for side in (1, 3):
            evict_y(which, side).wait_send()
    evicted = owner_ref[me] == oldest_ref[0]
    for h in range(HEADS):
        cols = slice(h * HD, (h + 1) * HD)
        moved_ref[0, :, cols] = jnp.where(evicted, moved_ref[0, :, cols], kbuf[y, h])
    moved_ref[1] = jnp.where(evicted, moved_ref[1], vbuf[...])
    store = pltpu.make_async_copy(moved_ref, new_hbm, new_sem)
    store.start()
    for i in range(1, NXC):
        return1_wait((xc + i) % NXC)
    gate = gate_ref[pl.ds(time_ref[0], 1), :]
    for s in range(NXC):
        pack32[s, 0:BACK1, :] = recv2[s].astype(F32)
        for half in range(2):
            for h in range(HEADS):
                row = (half * HEADS + h) * TOK
                col = ((half * NXC + s) * HEADS + h) * HD
                rows = pack32[s, row : row + TOK, :] * gate[:, col : col + HD]
                out_ref[:, col : col + HD] = rows.astype(BF)

    store.wait()
    for h in range(HEADS):
        for i in (1, 2, 3):
            quad_lse(h, (seat + i) % 4).wait_send()
            for slot in range(2):
                quad_part(h, slot, (seat + i) % 4).wait_send()
        for there, k in ways:
            for each in final_copies(h, k, there):
                each.wait_send()
    step2().wait_send()
    for i in range(3):
        seat_copy(i).wait_send()
    for i in range(4):
        for k in (1, 2, 3):
            quad_query(i, (seat + k) % 4).wait_send()
    for i in range(1, NXC):
        return1((xc + i) % NXC).wait_send()
    for i in (1, 3):
        a_copy(i).wait_send()
        for h in range(HEADS):
            k_copy(h, i).wait_send()
            v_copy(h, i).wait_send()
    for part, i in ((0, 1), (1, 3)):
        src = (y + NY - i) % NY
        a_relay(src, part).wait_send()
        for h in range(HEADS):
            for each in relay_copies(src, h, part):
                each.wait_send()
    for g in range(2):
        for half in range(2):
            @pl.when(evict_target(g, half) != z)
            def _():
                evict_z(g, half).wait_send()


def attention(x, window, owner, oldest, timestep, slopes, gate_table):
    dma = pltpu.SemaphoreType.DMA
    vm = pltpu.VMEM
    in_vmem = pl.BlockSpec(memory_space=pltpu.VMEM)
    in_any = pl.BlockSpec(memory_space=pl.ANY)
    return pl.pallas_call(
        kernel,
        out_shape=(
            jax.ShapeDtypeStruct((TOK, 2 * NXC * SHARE), BF),
            jax.ShapeDtypeStruct((2, CACHE, SHARE), BF),
        ),
        in_specs=[pl.BlockSpec(memory_space=pltpu.HBM)] * 7,
        out_specs=(in_vmem, in_any),
        scratch_shapes=[
            vm((3, TOK, 2 * NXC * SHARE), BF),
            vm((CACHE, SHARE), BF),
            vm((50, 2 * NXC * SHARE), F32),
            pltpu.SMEM((NZ * NY,), jnp.int32),
            pltpu.SMEM((1,), jnp.int32),
            pltpu.SMEM((1,), jnp.int32),
            pltpu.SMEM((2 * NXC * HEADS,), F32),
            vm((2, CACHE, SHARE), BF),
            dma((10,)), dma(()),
            vm((NXC, OUT1, HD), F32),
            vm((NXC, OUT1, HD), BF),
            vm((NXC, OUT1, HD), BF),
            vm((2, 3, HALF + 8, SHARE), F32),
            vm((NZ, ROWS, SHARE), BF),
            vm((NY, HEADS, CACHE, HD), BF),
            vm((NY, HEADS, SUMS, CACHE), BF),
            vm((NY, 2, ROWS, SHARE), BF),
            vm((HEADS, SUMS, PACK), BF),
            vm((SUMS, NZ * ROWS), F32),
            vm((8, NZ * ROWS), F32),
            vm((HEADS, 4, 2, ROWS, HD), BF),
            vm((HEADS, 4, 8, HD), F32),
            vm((HEADS, 4, 2, HD, HD), BF),
            vm((HEADS, 4, 8, HD), F32),
            vm((HEADS, 2, ROWS, HD), BF),
            vm((HEADS, 2, 8, HD), F32),
            vm((2, HEADS, 2, HD, HD), BF),
            vm((2, HEADS, 2, 8, HD), F32),
            vm((3, HALF, SHARE), BF),
            vm((NXC, BACK1, HD), BF),
            dma((NXC,)), dma((NXC,)),
            dma(()), dma(()),
            dma((3,)), dma((3,)), dma((4, 4)), dma((4, 4)),
            dma((NY, HEADS)), dma((NY, HEADS)), dma((NY, HEADS)), dma((NY, HEADS)),
            dma((2, HEADS)), dma((2, HEADS)), dma((2, HEADS)), dma((2, HEADS)),
            dma((NY,)), dma((NY,)), dma((2,)), dma((2,)),
            dma((HEADS, 2, 4)), dma((HEADS, 2, 4)), dma((HEADS, 4)), dma((HEADS, 4)),
            dma((HEADS, 3)), dma((2, HEADS, 2)), dma((HEADS, 3)), dma((2, HEADS, 2)),
            dma((2, 2)), dma((2, 2)), dma((2, NY)), dma((2, NY)),
            dma((2,)), dma((2,)),
            dma((NXC,)), dma((NXC,)), dma(()),
        ],
        compiler_params=pltpu.CompilerParams(
            collective_id=0, has_side_effects=True, vmem_limit_bytes=60 * 1024 * 1024
        ),
        cost_estimate=pl.CostEstimate(
            flops=4 * 3072 * 864 * SHARE, bytes_accessed=4 * 2**20, transcendentals=3072 * 864 * 3
        ),
    )(x, window, owner, oldest, timestep, slopes, gate_table)


def closing(attended_in, new_in, attended_out, new_out, attended, new, sem):
    parts = [(attended_in, attended, attended_out)]
    for half in range(2):
        for part in range(2):
            rows = pl.ds(part * PACK, PACK)
            parts.append(
                tuple(ref.at[half, rows, :] for ref in (new_in, new, new_out))
            )
    loads = [
        pltpu.make_async_copy(src, held, sem.at[0, i]) for i, (src, held, _) in enumerate(parts)
    ]
    stores = [
        pltpu.make_async_copy(held, dst, sem.at[1, i]) for i, (_, held, dst) in enumerate(parts)
    ]
    for load in loads:
        load.start()
    for load, store in zip(loads, stores):
        load.wait()
        store.start()
    for store in stores:
        store.wait()


def close(attended, new):
    in_hbm = pl.BlockSpec(memory_space=pltpu.HBM)
    return pl.pallas_call(
        closing,
        out_shape=tuple(jax.ShapeDtypeStruct(a.shape, a.dtype) for a in (attended, new)),
        in_specs=[in_hbm] * 2,
        out_specs=[in_hbm] * 2,
        scratch_shapes=[
            pltpu.VMEM(attended.shape, attended.dtype),
            pltpu.VMEM(new.shape, new.dtype),
            pltpu.SemaphoreType.DMA((2, 5)),
        ],
        compiler_params=pltpu.CompilerParams(vmem_limit_bytes=60 * 1024 * 1024),
    )(attended, new)


def body(active_qkv, window_kv, slot_owner, oldest_slot, timestep, time_slopes, gate_table):
    attended, new_window = attention(
        active_qkv, window_kv, slot_owner, oldest_slot, timestep, time_slopes, gate_table
    )
    return close(attended, new_window)


def solution(mesh):
    in_specs = (P(None, ("grp", "sp"), None), P(None, "grp", "sp"), P(), P(), P(), P(), P())
    out_specs = (P(("grp", "sp"), None), P(None, "grp", "sp"))
    return jax.shard_map(body, mesh=mesh, in_specs=in_specs, out_specs=out_specs, check_vma=False)
```
